32 devices in a mesh: groups: 2 (over x), row: 16 (over z, y, core).
Axes of the slice: x: 2, y: 2, z: 4, core: 2. Of those that a mesh axis runs over, the one named last changes fastest.
Arguments:
- panels: bfloat16 [512, 6, 64, 128], P(('groups', 'row')), parts along dimension 0, may hold values from -1 to 1
- blocks: int32 [512, 6], P(('groups', 'row')), parts along dimension 0, may hold values from 0 to 15, all different within a row; in each aligned block of 16 rows (0 to 15, 16 to 31, ...) at most 6 rows name the same one
- row_block: int32 [32], P('groups'), parts along dimension 0, may hold values from 0 to 15, each once
- coeffs: float32 [512, 6, 128], P(('groups', 'row')), parts along dimension 0, may hold values from -0.109375 to 0.109375
- metric_inv: float32 [128, 64], P('groups'), parts along dimension 0, may hold values from -1 to 3, as said below
- three_index: bfloat16 [32, 64, 128, 128], P(('groups', 'row')), parts along dimension 0, may hold values from -0.75 to 0.75
Outputs:
- exchange: bfloat16 [32, 128, 2048], P(('groups', 'row')), parts along dimension 0
- coulomb: bfloat16 [32, 128, 128], P(('groups', 'row')), parts along dimension 0
- fitted: float32 [128], P('groups'), parts along dimension 0
The draws below stay inside these ranges and needn't reach their ends.
There are 2 independent parts, one for each index of `groups`. The reference program is written for one: setup_inputs(seed, part) draws one part's arguments, and reference() takes and returns one part's arrays. A program takes and returns all parts, laid end to end along the dimension named above; each array names one. Nothing has to cross between parts.
Inputs may be any that keep to these rules, and one draw needn't show every extreme that they name: Each orbital names 6 different blocks; among the orbitals of one device (aligned runs of 16 orbitals) no block is named more than 6 times, and that bound is reached. `row_block`: each block appears once. `metric_inv`: Symmetric.
All inputs are finite; a program needn't handle non-finite values.
Results may differ from the reference program's by a relative error of at most 0.001.
Values may be sent and summed in bfloat16 or wider, within the bound.
No kernel may reach another device: no remote copies, remote signals or barrier semaphores. Data moves between devices by JAX's collectives and lax.ppermute only.
A program may use at most 192 MiB of HBM per device.

```python
import math
import jax
import jax.numpy as jnp
import numpy as np
from jax import lax

BS = 128
AUX = 64
SLOTS = 6
ORB_DEV = 16
NB = 16
CAP = 6
ORBS = 256


def draw_metric_inv(key, part):
    key = jax.random.fold_in(key, 7)
    first, second = jax.random.split(key)
    spread = jax.random.normal(first, (AUX, AUX), jnp.float32)
    offdiag = (spread + spread.T) * (0.3 / AUX ** 0.5)
    diag = jax.random.uniform(second, (AUX,), jnp.float32, 1.5, 3.0)
    ident = jnp.arange(AUX)[:, None] == jnp.arange(AUX)[None, :]
    return jnp.where(ident, diag[None, :], offdiag)


def level_of(own_key, dims, pieces, least, high):
    gain = 1.0
    for axis_at, shards_of in pieces:
        draws = jax.random.uniform(jax.random.fold_in(jax.random.fold_in(own_key, 6), axis_at), (shards_of,), jnp.float32, least / len(pieces), high / len(pieces))
        gain = gain * jnp.repeat(jnp.exp(draws), dims[axis_at] // shards_of).reshape((-1,) + (1,) * (len(dims) - 1 - axis_at))
    return gain


def assign_block(stream_key, own, number, rows, count, top, bound, lean):
    sequence = jax.random.permutation(stream_key, count)
    crowded, common = load_shares(count, rows * top, bound, lean, True), load_shares(count, rows * top, bound, lean, False)
    places = jnp.arange(count)

    def named(sizes, turn):
        used = int((sizes > 0).sum())
        fixed = max(1, used // 4)
        passed = fixed + (places - fixed + turn * (used - fixed)) % max(1, count - fixed)
        return jnp.zeros((count,), jnp.int32).at[sequence[jnp.where(places < fixed, places, passed)]].set(jnp.asarray(sizes, jnp.int32))

    sizes = jnp.where(number % 4 == 0, named(crowded, number // 4), named(common, number - number // 4 - 1))
    mixed = jax.random.permutation(jax.random.fold_in(own, 3), count)
    donor, receiver = mixed[0:count // 2 * 2:2], mixed[1:count // 2 * 2:2]
    slack = jnp.minimum(sizes[donor] - 1, bound - sizes[receiver]) // 2
    slack = jnp.where((donor == sequence[0]) | (receiver == sequence[0]) | (sizes[receiver] == 0), 0, jnp.maximum(slack, 0))
    passed = jax.random.randint(jax.random.fold_in(own, 4), (count // 2,), 0, 1 << 20) % (slack + 1)
    sizes = sizes.at[donor].add(-passed).at[receiver].add(passed)
    members = jnp.searchsorted(jnp.cumsum(sizes), jnp.arange(rows * top), side="right").astype(jnp.int32)
    listing = members.reshape(top, rows).T
    listing = listing[jax.random.permutation(jax.random.fold_in(own, 1), rows)]
    turn = jax.random.randint(jax.random.fold_in(own, 2), (rows, 1), 0, top)
    return jnp.take_along_axis(listing, (jnp.arange(top)[None, :] + turn) % top, axis=1)


def load_shares(number_of, total, limit, skew, full):
    portions = [(1 << 20) // math.isqrt(grade ** skew) + 1 for grade in range(1, number_of + 1)]
    largest = limit if full else min(limit, max(-(-total // number_of), total * portions[0] // sum(portions)))
    least = 1 if total - largest >= number_of - 1 else 0
    given, surplus = [largest] + [least] * (number_of - 1), total - largest - least * (number_of - 1)
    while surplus > 0:
        candidates = [i for i in range(1, number_of) if given[i] < largest] or [i for i in range(1, number_of) if given[i] < limit]
        mass, budget = sum([portions[i] for i in candidates]), surplus
        for i in candidates:
            addition = min(limit - given[i], max(1, budget * portions[i] // mass), surplus)
            given[i] = given[i] + addition
            surplus = surplus - addition
    return np.array(given)


def centred(stream_key, dims, deviation, most, pieces=(), dtype=jnp.bfloat16):
    drawn = jax.random.normal(stream_key, dims, jnp.float32) * deviation
    if len(pieces) > 0:
        drawn = level_of(stream_key, dims, pieces, -0.22, 0.18) * drawn
    return jnp.clip(drawn, min=-most, max=most).astype(dtype)


def setup_inputs(seed: int = 0, part: int = 0) -> dict:
    keys = jax.random.split(jax.random.key(seed), 7)
    part_keys = jax.random.split(jax.random.fold_in(keys[6], part), 7)
    panels = centred(part_keys[0], (ORBS, SLOTS, AUX, BS), 0.125, 1.0, ((0, 16),))
    blocks_keys = jax.random.split(jax.random.fold_in(part_keys[1], 1), ORBS // ORB_DEV)
    blocks_turns = jax.random.permutation(jax.random.fold_in(part_keys[1], 3), ORBS // ORB_DEV)
    blocks = jax.vmap(lambda own, number: assign_block(jax.random.fold_in(part_keys[1], 2), own, number, ORB_DEV, NB, SLOTS, CAP, 2))(blocks_keys, blocks_turns).reshape((ORBS, SLOTS))
    row_block = jax.random.permutation(part_keys[2], NB).astype(jnp.int32)
    coeffs = centred(part_keys[3], (ORBS, SLOTS, BS), (NB * ORB_DEV * SLOTS * BS // 64) ** -0.5, 0.109375, ((0, 16),), jnp.float32)
    metric_inv = draw_metric_inv(jax.random.fold_in(jax.random.fold_in(keys[6], part), 71), part)
    three_index = centred(part_keys[5], (NB, AUX, BS, BS), AUX ** -0.5, 0.75, ((0, 16),))
    return {"panels": panels, "blocks": blocks, "row_block": row_block, "coeffs": coeffs, "metric_inv": metric_inv, "three_index": three_index}


def reference(panels, blocks, row_block, coeffs, metric_inv, three_index):
    group = 8
    total_orbs = panels.shape[0]
    grouped = panels.reshape(total_orbs // group, group, SLOTS, AUX, BS)
    grouped_ids = blocks.reshape(total_orbs // group, group, SLOTS)

    def step(total, item):
        block_rows, block_ids = item
        floated = block_rows.astype(jnp.float32)
        prods = jnp.einsum('ispm,itpn->istmn', floated, floated)
        rows_at = jnp.broadcast_to(block_ids[:, :, None], (group, SLOTS, SLOTS))
        cols_at = jnp.broadcast_to(block_ids[:, None, :], (group, SLOTS, SLOTS))
        return total.at[rows_at, :, cols_at, :].add(prods), None

    start = jnp.zeros((NB, BS, NB, BS), jnp.float32)
    matrix, _ = lax.scan(step, start, (grouped, grouped_ids))
    exchange = matrix[row_block.astype(jnp.int32)].reshape(NB, BS, NB * BS).astype(jnp.bfloat16)
    gamma = jnp.einsum('ispm,ism->p', panels.astype(jnp.float32), coeffs, precision=lax.Precision.HIGHEST)
    fitted = jnp.dot(metric_inv, gamma, precision=lax.Precision.HIGHEST)
    coulomb = jnp.einsum('p,rpmn->rmn', fitted, three_index.astype(jnp.float32), precision=lax.Precision.HIGHEST)
    return exchange, coulomb.astype(jnp.bfloat16), fitted
```

```python
import functools
import jax
import jax.numpy as jnp
from jax import lax
from jax.experimental import pallas as pl
from jax.experimental.pallas import tpu as pltpu
from jax.sharding import PartitionSpec as P


def row_terms(rows_in, row_ids, owned, count):
    total_rows = rows_in.shape[0]
    group = 32
    slots = rows_in.shape[1]
    width = rows_in.shape[3]
    grouped = rows_in.reshape((total_rows // group, group) + rows_in.shape[1:])
    grouped_ids = row_ids.reshape(total_rows // group, group, slots)

    def step(total, item):
        block_rows, block_ids = item
        chosen = (block_ids == owned).astype(jnp.bfloat16)
        picked = jnp.einsum(
            "gs,gspk->gpk", chosen, block_rows, preferred_element_type=jnp.float32
        ).astype(jnp.bfloat16)
        prods = jnp.einsum("gpk,gspn->gskn", picked, block_rows, preferred_element_type=jnp.float32)
        target = jnp.maximum(block_ids, 0).reshape(-1)
        added = jax.ops.segment_sum(prods.reshape(-1, width, width), target, num_segments=count)
        return (total + added, None)

    start = jnp.zeros((count, width, width), jnp.float32)
    total, _ = lax.scan(step, start, (grouped, grouped_ids))
    return total


def sent_panels(panels, blocks, row_block, coeffs, metric_inv, three_index):
    count = row_block.shape[0]
    orbits, slots, aux, width = panels.shape
    capacity = max(2, (orbits * slots + count - 1) // count)
    here = lax.axis_index("row")
    owned = row_block[here]
    ranks = jnp.arange(count, dtype=jnp.int32)
    flat_ids = blocks.reshape(-1)
    matches = (row_block[None, :] == flat_ids[:, None]).astype(jnp.int32)
    target = jnp.sum(matches * ranks[None, :], axis=1)
    hits = (ranks[None, :] == target[:, None]).astype(jnp.int32)
    before = jnp.cumsum(hits, axis=0) - hits
    place = jnp.sum(before * hits, axis=1)
    source = jnp.repeat(panels, slots, axis=0)
    source_ids = jnp.repeat(blocks, slots, axis=0).astype(jnp.bfloat16)
    outgoing = (
        jnp.zeros((count, capacity, slots, aux, width), jnp.bfloat16).at[target, place].set(source)
    )
    outgoing_ids = (
        jnp.full((count, capacity, slots), -1.0, jnp.bfloat16).at[target, place].set(source_ids)
    )
    partial_terms = jnp.einsum(
        "ispm,ism->p", panels.astype(jnp.float32), coeffs, precision=lax.Precision.HIGHEST
    )
    gamma = lax.psum(partial_terms, "row")
    fitted = jnp.dot(metric_inv, gamma, precision=lax.Precision.HIGHEST)
    coulomb = jnp.einsum(
        "p,rpmn->rmn", fitted, three_index.astype(jnp.float32), precision=lax.Precision.HIGHEST
    )
    arrived, arrived_ids = (
        lax.all_to_all(outgoing, "row", split_axis=0, concat_axis=0, tiled=True),
        lax.all_to_all(outgoing_ids, "row", split_axis=0, concat_axis=0, tiled=True),
    )
    accum = row_terms(
        arrived.reshape(-1, slots, aux, width),
        arrived_ids.reshape(-1, slots).astype(jnp.int32),
        owned,
        count,
    )
    exchange = accum.transpose(1, 0, 2).reshape(width, count * width)[None].astype(jnp.bfloat16)
    return (exchange, coulomb.astype(jnp.bfloat16), fitted)


DEPTH = 4
ROWS = 4 * DEPTH
HALF = ROWS // 2
Z_FIRST = ((1, 3),)
Y_FIRST = ((4, 5), (0, 1))


def piece_of(z, k):
    inner = jnp.where(k < 2, 3 - k, k - 2)
    return jnp.where(z == 0, 3 - k, jnp.where(z == 3, k, jnp.where(z == 1, inner, 3 - inner)))


def dense_kernel(runs, y_major, holders_ref, mine_ids, other_ids, mine, other, out, rank_of, dense):
    orbits, slots, aux, width = mine.shape
    step = pl.program_id(0)
    me = lax.axis_index("row")

    @pl.when(step == 0)
    def _():
        for k in range(ROWS):
            rank_of[holders_ref[k]] = k
        dense[...] = jnp.zeros_like(dense)

        def place(i, carry):
            for which, (ids, rows) in enumerate(((mine_ids, mine), (other_ids, other))):
                at = pl.ds(pl.multiple_of((which * orbits + i) * aux, aux), aux)
                for s in range(slots):
                    rank = rank_of[ids[i, s]]
                    tile = rows[i, s]
                    dense[at, pl.ds(pl.multiple_of(rank * width, width), width)] = tile
                    again = jnp.where(rank < HALF, rank + ROWS, rank)
                    dense[at, pl.ds(pl.multiple_of(again * width, width), width)] = tile
            return carry

        lax.fori_loop(0, orbits, place, 0)

    if y_major:
        y, k = step // DEPTH, step % DEPTH
    else:
        k, y = step // 2, step % 2
    row = piece_of(me // 4, k) * 4 + y * 2 + me % 2
    left = dense[:, pl.ds(pl.multiple_of(row * width, width), width)]
    at = 0
    for first, number in runs:
        right = dense[:, pl.ds(pl.multiple_of((row + first) * width, width), number * width)]
        out[0, 0, :, at : at + number * width] = lax.dot_general(
            left, right, (((0,), (0,)), ((), ())), preferred_element_type=jnp.float32
        )
        at += number * width


def partial_rows(runs, y_major, row_block, mine_ids, other_ids, mine, other):
    orbits, slots, aux, width = mine.shape
    columns = sum(number for _, number in runs) * width
    outer, inner = (2, DEPTH) if y_major else (DEPTH, 2)
    scalars = pl.BlockSpec(memory_space=pltpu.SMEM)
    whole = pl.BlockSpec(mine.shape, lambda g: (0, 0, 0, 0))
    flops = 2 * outer * inner * width * columns * 2 * orbits * aux
    return pl.pallas_call(
        functools.partial(dense_kernel, runs, y_major),
        grid=(outer * inner,),
        in_specs=[scalars, scalars, scalars, whole, whole],
        out_specs=pl.BlockSpec((1, 1, width, columns), lambda g: (g // inner, g % inner, 0, 0)),
        out_shape=jax.ShapeDtypeStruct((outer, inner, width, columns), jnp.float32),
        scratch_shapes=[
            pltpu.SMEM((ROWS,), jnp.int32),
            pltpu.VMEM((2 * orbits * aux, (ROWS + HALF) * width), jnp.bfloat16),
        ],
        compiler_params=pltpu.CompilerParams(vmem_limit_bytes=48 << 20),
        cost_estimate=pl.CostEstimate(
            flops=flops, bytes_accessed=4 * outer * inner * width * columns, transcendentals=0
        ),
    )(row_block, mine_ids, other_ids, mine, other)


def pairs(move):
    return [(i, move(i)) for i in range(ROWS) if move(i) is not None]


ACROSS_CORE = pairs(lambda i: i ^ 1)
ACROSS_Y = pairs(lambda i: i ^ 2)


def rightward(upto):
    return [(i, i + 4) for i in range(ROWS) if i // 4 <= upto and i // 4 < 3]


def leftward(upto):
    return [(i, i - 4) for i in range(ROWS) if 3 - i // 4 <= upto and i // 4 > 0]


def sum_along_z(pieces, z):
    ends = (z == 0) | (z == DEPTH - 1)
    came = lax.ppermute(pieces[0], "row", rightward(0) + leftward(0))
    going = jnp.where(ends, pieces[1], pieces[0]) + came
    right = lax.ppermute(going, "row", rightward(1))
    left = lax.ppermute(going, "row", leftward(1))
    right = lax.ppermute(jnp.where(z == 1, pieces[1], pieces[2]) + right, "row", rightward(2))
    left = lax.ppermute(jnp.where(z == 2, pieces[1], pieces[2]) + left, "row", leftward(2))
    return pieces[3] + right + left


def summed_rows(panels, blocks, row_block, coeffs, metric_inv, three_index):
    width = panels.shape[3]
    me = lax.axis_index("row")
    z, y = me // 4, (me // 2) % 2

    other = lax.ppermute(panels, "row", ACROSS_CORE)
    other_ids = lax.ppermute(blocks, "row", ACROSS_CORE)

    gamma = jnp.einsum(
        "ispm,ism->p", panels.astype(jnp.float32), coeffs, precision=lax.Precision.HIGHEST
    )
    for bit in (1, 2, 4, 8):
        gamma = gamma + lax.ppermute(gamma, "row", pairs(lambda i: i ^ bit))
    fitted = jnp.dot(metric_inv, gamma, precision=lax.Precision.HIGHEST)
    coulomb = jnp.einsum(
        "p,rpmn->rmn", fitted, three_index.astype(jnp.float32), precision=lax.Precision.HIGHEST
    )

    z_first = partial_rows(Z_FIRST, False, row_block, blocks, other_ids, panels, other)
    y_first = partial_rows(Y_FIRST, True, row_block, blocks, other_ids, panels, other)

    own = lax.dynamic_index_in_dim(y_first, y, 0, keepdims=False)
    theirs = lax.dynamic_index_in_dim(y_first, 1 - y, 0, keepdims=False)
    pieces = [own[k] + lax.ppermute(theirs[k], "row", ACROSS_Y) for k in range(DEPTH)]
    late = sum_along_z(pieces, z)

    early = sum_along_z([z_first[k] for k in range(DEPTH)], z)
    early = lax.dynamic_index_in_dim(early, y, 0, keepdims=False) + lax.ppermute(
        lax.dynamic_index_in_dim(early, 1 - y, 0, keepdims=False), "row", ACROSS_Y
    )

    held = {}
    for runs, rows in ((Z_FIRST, early), (Y_FIRST, late)):
        at = 0
        for first, number in runs:
            for d in range(first, first + number):
                held[d] = rows[:, at * width : (at + 1) * width].astype(jnp.bfloat16)
                at += 1
    ring = [held[d] for d in range(HALF + 1)]
    for d in range(HALF - 1, 0, -1):
        ring.append(lax.ppermute(held[d].T, "row", pairs(lambda i: (i + d) % ROWS)))
    place = (row_block[:, None] == jnp.arange(ROWS)[None, :]).astype(jnp.int32)
    source = (jnp.sum(place * jnp.arange(ROWS)[:, None], axis=0) - me) % ROWS
    exchange = jnp.stack(ring)[source].transpose(1, 0, 2).reshape(1, width, ROWS * width)
    return (exchange, coulomb.astype(jnp.bfloat16), fitted)


def solution(mesh):
    placed = (
        P(("groups", "row"), None, None, None),
        P(("groups", "row"), None),
        P("groups"),
        P(("groups", "row"), None, None),
        P("groups", None),
        P(("groups", "row"), None, None, None),
    )
    return jax.shard_map(
        summed_rows if mesh.shape["row"] == ROWS else sent_panels,
        mesh=mesh,
        in_specs=placed,
        out_specs=(P(("groups", "row"), None, None), P(("groups", "row"), None, None), P("groups")),
        check_vma=False,
    )
```

```python
import functools
import jax
import jax.numpy as jnp
from jax import lax
from jax.experimental import pallas as pl
from jax.experimental.pallas import tpu as pltpu
from jax.sharding import PartitionSpec as P


def row_terms(rows_in, row_ids, owned, count):
    total_rows = rows_in.shape[0]
    group = 32
    slots = rows_in.shape[1]
    width = rows_in.shape[3]
    grouped = rows_in.reshape((total_rows // group, group) + rows_in.shape[1:])
    grouped_ids = row_ids.reshape(total_rows // group, group, slots)

    def step(total, item):
        block_rows, block_ids = item
        chosen = (block_ids == owned).astype(jnp.bfloat16)
        picked = jnp.einsum(
            "gs,gspk->gpk", chosen, block_rows, preferred_element_type=jnp.float32
        ).astype(jnp.bfloat16)
        prods = jnp.einsum("gpk,gspn->gskn", picked, block_rows, preferred_element_type=jnp.float32)
        target = jnp.maximum(block_ids, 0).reshape(-1)
        added = jax.ops.segment_sum(prods.reshape(-1, width, width), target, num_segments=count)
        return (total + added, None)

    start = jnp.zeros((count, width, width), jnp.float32)
    total, _ = lax.scan(step, start, (grouped, grouped_ids))
    return total


def sent_panels(panels, blocks, row_block, coeffs, metric_inv, three_index):
    count = row_block.shape[0]
    orbits, slots, aux, width = panels.shape
    capacity = max(2, (orbits * slots + count - 1) // count)
    here = lax.axis_index("row")
    owned = row_block[here]
    ranks = jnp.arange(count, dtype=jnp.int32)
    flat_ids = blocks.reshape(-1)
    matches = (row_block[None, :] == flat_ids[:, None]).astype(jnp.int32)
    target = jnp.sum(matches * ranks[None, :], axis=1)
    hits = (ranks[None, :] == target[:, None]).astype(jnp.int32)
    before = jnp.cumsum(hits, axis=0) - hits
    place = jnp.sum(before * hits, axis=1)
    source = jnp.repeat(panels, slots, axis=0)
    source_ids = jnp.repeat(blocks, slots, axis=0).astype(jnp.bfloat16)
    outgoing = (
        jnp.zeros((count, capacity, slots, aux, width), jnp.bfloat16).at[target, place].set(source)
    )
    outgoing_ids = (
        jnp.full((count, capacity, slots), -1.0, jnp.bfloat16).at[target, place].set(source_ids)
    )
    partial_terms = jnp.einsum(
        "ispm,ism->p", panels.astype(jnp.float32), coeffs, precision=lax.Precision.HIGHEST
    )
    gamma = lax.psum(partial_terms, "row")
    fitted = jnp.dot(metric_inv, gamma, precision=lax.Precision.HIGHEST)
    coulomb = jnp.einsum(
        "p,rpmn->rmn", fitted, three_index.astype(jnp.float32), precision=lax.Precision.HIGHEST
    )
    arrived, arrived_ids = (
        lax.all_to_all(outgoing, "row", split_axis=0, concat_axis=0, tiled=True),
        lax.all_to_all(outgoing_ids, "row", split_axis=0, concat_axis=0, tiled=True),
    )
    accum = row_terms(
        arrived.reshape(-1, slots, aux, width),
        arrived_ids.reshape(-1, slots).astype(jnp.int32),
        owned,
        count,
    )
    exchange = accum.transpose(1, 0, 2).reshape(width, count * width)[None].astype(jnp.bfloat16)
    return (exchange, coulomb.astype(jnp.bfloat16), fitted)


ROWS = 16
CORE, Y, Z = 1, 2, (4, 8, 12)
PLACES = 16
Z_FIRST, Y_FIRST = (1, "extra"), (2, 3, 0)
TAIL = 16
TOP = 14.99


def send(x, flip):
    return lax.ppermute(x, "row", [(i, i ^ flip) for i in range(ROWS)])


def swap_low(index):
    return (index & 12) | ((index & 1) << 1) | ((index >> 1) & 1)


def side_of(z, apart):
    return (z >> 1) & 1 if apart == 2 else z & 1


def first_place(row, region):
    if region == 0:
        return 0
    if region == "extra":
        return 2 + (row & 1)
    return region * 4 + side_of(row >> 2, region) * 2


def width_of(region):
    return 1 if region == "extra" else 2


def encode(out, sums):
    height, columns = sums[0].shape
    line = lax.broadcasted_iota(jnp.int32, (TAIL, columns), 0)
    exponents = jnp.zeros((TAIL, columns), jnp.float32)
    for j, x in enumerate(sums):
        peak = jnp.maximum(jnp.max(jnp.abs(x), axis=0, keepdims=True), 2.0**-100)
        exponent = jnp.ceil(jnp.log2(peak) * 8)
        scaled = jnp.round(x * jnp.exp2(TOP - exponent * 0.125))
        out[j * height : (j + 1) * height, :] = scaled.astype(jnp.int32).astype(jnp.int16)
        exponents = jnp.where(line == j, exponent, exponents)
    out[len(sums) * height :, :] = exponents.astype(jnp.int32).astype(jnp.int16)


def decode(codes, j, height):
    count = (codes.shape[0] - TAIL) // height
    exponents = codes[count * height :, :].astype(jnp.int32).astype(jnp.float32)
    scale = jnp.exp2(exponents[j : j + 1, :] * 0.125 - TOP)
    return codes[j * height : (j + 1) * height, :].astype(jnp.int32).astype(jnp.float32) * scale


def rows_kernel(group, flips, per_message, sides, *refs):
    lists, ranks, panels = refs[:sides], refs[sides : 2 * sides], refs[2 * sides : 3 * sides]
    outs, picks, spreads = refs[3 * sides : -4], refs[-4:-2], refs[-2:]
    orbits, slots, aux, width = panels[0].shape
    capacity = lists[0].shape[1]
    me = lax.axis_index("row")
    gathered = []

    for j, flip in enumerate(flips):
        row = me ^ flip
        row_rank = swap_low(row)
        picked, spread = picks[j % 2], spreads[j % 2]
        spans = [
            pl.ds(pl.multiple_of(first_place(row, region) * width, width), width_of(region) * width)
            for region in group
        ]
        for span in spans:
            spread[:, span] = jnp.zeros((spread.shape[0], span.size), jnp.bfloat16)
        for side in range(sides):
            for n in range(capacity):
                code = lists[side][row, n]
                orbit, slot = jnp.maximum(code, 0) >> 3, jnp.maximum(code, 0) & 7
                at = pl.ds((side * capacity + n) * aux, aux)
                chosen = panels[side][orbit, slot]
                tiles = [panels[side][orbit, t] for t in range(slots)]
                places = [ranks[side][orbit, t] ^ row_rank for t in range(slots)]
                picked[at, :] = jnp.where(code >= 0, chosen, jnp.zeros_like(chosen))
                for tile, place in zip(tiles, places):
                    spread[at, pl.ds(pl.multiple_of(place * width, width), width)] = tile
        sums = [
            lax.dot_general(
                picked[...],
                spread[:, span],
                (((0,), (0,)), ((), ())),
                preferred_element_type=jnp.float32,
            )
            for span in spans
        ]
        if per_message:
            gathered.append(jnp.concatenate(sums, axis=1))
            if len(gathered) == per_message:
                encode(outs[j // per_message], gathered)
                gathered = []
        else:
            at = 0
            for x in sums:
                outs[0][j, :, at : at + x.shape[1]] = x
                at += x.shape[1]


def partial_rows(group, flips, per_message, lists, ranks, panels):
    orbits, slots, aux, width = panels[0].shape
    capacity, sides = lists[0].shape[1], len(panels)
    columns = sum(width_of(region) for region in group) * width
    depth = sides * capacity * aux
    if per_message:
        message = jax.ShapeDtypeStruct((per_message * width + TAIL, columns), jnp.int16)
        shapes = [message] * (len(flips) // per_message)
    else:
        shapes = [jax.ShapeDtypeStruct((len(flips), width, columns), jnp.float32)]
    scalars = pl.BlockSpec(memory_space=pltpu.SMEM)
    whole = pl.BlockSpec(memory_space=pltpu.VMEM)
    return pl.pallas_call(
        functools.partial(rows_kernel, group, flips, per_message, sides),
        in_specs=[scalars] * (2 * sides) + [whole] * sides,
        out_specs=[whole] * len(shapes),
        out_shape=shapes,
        scratch_shapes=[pltpu.VMEM((depth, width), jnp.bfloat16)] * 2
        + [pltpu.VMEM((depth, PLACES * width), jnp.bfloat16)] * 2,
        compiler_params=pltpu.CompilerParams(vmem_limit_bytes=32 << 20),
        cost_estimate=pl.CostEstimate(
            flops=8 * len(flips) * width * columns * depth,
            bytes_accessed=4 * len(flips) * width * columns,
            transcendentals=0,
        ),
    )(*lists, *ranks, *panels)


def turn_y_kernel(stay, along_z, message, own, *codes):
    height = own.shape[0]
    rows = [stay[j] + sum(decode(c, j, height) for c in codes) for j in range(2)]
    encode(message, rows[:1])
    own[...] = rows[1]


def turn_y(stay, codes):
    height, columns = stay.shape[1:]
    return pl.pallas_call(
        lambda stay, *refs: turn_y_kernel(stay, None, refs[-2], refs[-1], *refs[:-2]),
        out_shape=[
            jax.ShapeDtypeStruct((height + TAIL, columns), jnp.int16),
            jax.ShapeDtypeStruct((height, columns), jnp.float32),
        ],
        compiler_params=pltpu.CompilerParams(vmem_limit_bytes=32 << 20),
    )(stay, *codes)


def turn_z_kernel(stay, code, *outs):
    height = stay.shape[1]
    for j in range(1, len(outs)):
        encode(outs[j], [stay[j] + decode(code, j, height)])
    outs[0][...] = stay[0] + decode(code, 0, height)


def turn_z(stay, code):
    count, height, columns = stay.shape
    message = jax.ShapeDtypeStruct((height + TAIL, columns), jnp.int16)
    return pl.pallas_call(
        turn_z_kernel,
        out_shape=[jax.ShapeDtypeStruct((height, columns), jnp.float32)] + [message] * (count - 1),
        compiler_params=pltpu.CompilerParams(vmem_limit_bytes=32 << 20),
    )(stay, code)


def finish_kernel(backs, own, *refs):
    codes, done, back = refs[: -backs - 1], refs[-backs - 1], refs[len(refs) - backs :]
    height = own.shape[0]
    total = own[...] + sum(decode(c, 0, height) for c in codes)
    done[...] = total.astype(jnp.bfloat16)
    for b, out in enumerate(back):
        out[...] = total[:, b * height : (b + 1) * height].T.astype(jnp.bfloat16)


def finish(own, codes, backs):
    height, columns = own.shape
    return pl.pallas_call(
        functools.partial(finish_kernel, backs),
        out_shape=[jax.ShapeDtypeStruct((height, columns), jnp.bfloat16)]
        + [jax.ShapeDtypeStruct((height, height), jnp.bfloat16)] * backs,
        compiler_params=pltpu.CompilerParams(vmem_limit_bytes=32 << 20),
    )(own, *codes)


def give_back(block, region, b):
    def holder(i):
        return i ^ swap_low(first_place(i, region) + b)

    return lax.ppermute(block, "row", [(i, holder(i)) for i in range(ROWS)])


def assemble_kernel(holders, early, late, *refs):
    came, out = refs[:-1], refs[-1]
    width = early.shape[0]
    me = lax.axis_index("row")
    rank = swap_low(me)

    def put(place, block):
        column = holders[swap_low(place ^ rank)]
        out[0, :, pl.ds(pl.multiple_of(column * width, width), width)] = block

    k = 0
    for group, rows in ((Z_FIRST, early), (Y_FIRST, late)):
        at = 0
        for region in group:
            start = first_place(me, region)
            for b in range(width_of(region)):
                put(start + b, rows[:, at * width : (at + 1) * width])
                at += 1
                if region == 0:
                    continue
                other = 5 - start if region == "extra" else region * 8 + 2 - start + b
                put(other, came[k][...])
                k += 1


def assemble(row_block, early, late, came):
    width = early.shape[0]
    vmem = pl.BlockSpec(memory_space=pltpu.VMEM)
    return pl.pallas_call(
        assemble_kernel,
        in_specs=[pl.BlockSpec(memory_space=pltpu.SMEM)] + [vmem] * (2 + len(came)),
        out_shape=jax.ShapeDtypeStruct((1, width, ROWS * width), jnp.bfloat16),
    )(row_block, early, late, *came)


def naming(blocks, row_block, capacity):
    orbits, slots = blocks.shape
    holders = jnp.arange(ROWS, dtype=jnp.int32)
    hits = (blocks[:, :, None] == row_block[None, None, :]).astype(jnp.int32)
    rank = jnp.sum(hits * swap_low(holders), axis=2)
    named = jnp.sum(hits, axis=1)
    code = jnp.arange(orbits, dtype=jnp.int32)[:, None] * 8 + jnp.sum(
        hits * jnp.arange(slots, dtype=jnp.int32)[None, :, None], axis=1
    )
    earlier = (jnp.arange(orbits)[None, :] < jnp.arange(orbits)[:, None]).astype(jnp.int32)
    before = jnp.sum(earlier[:, :, None] * named[None, :, :], axis=1)
    here = (before[:, :, None] == jnp.arange(capacity)) & (named[:, :, None] > 0)
    listed = jnp.sum(jnp.where(here, code[:, :, None] + 1, 0), axis=0) - 1
    return listed, rank


def summed_rows(panels, blocks, row_block, coeffs, metric_inv, three_index):
    orbits, slots, aux, width = panels.shape
    capacity = orbits * slots // ROWS

    other = send(panels, CORE)
    listed, rank = naming(blocks, row_block, capacity)
    listed_other, rank_other = send(listed, CORE), send(rank, CORE)
    rest = ((listed, listed_other), (rank, rank_other), (panels, other))
    gamma = jnp.einsum(
        "ispm,ism->p", panels.astype(jnp.float32), coeffs, precision=lax.Precision.HIGHEST
    )
    gamma = gamma + send(gamma, CORE)

    early_go = partial_rows(Z_FIRST, [z | y for z in Z for y in (Y, 0)], 2, *rest)
    *early_go, gamma = lax.optimization_barrier((*early_go, gamma))
    near, far, across = [send(gamma, z) for z in Z]
    gamma = (gamma + near) + (far + across)
    early_codes = [send(x, z) for x, z in zip(early_go, Z)]
    (late_go,) = partial_rows(Y_FIRST, [Y] + [z | Y for z in Z], 4, *rest)
    late_go, gamma = lax.optimization_barrier((late_go, gamma))
    gamma = gamma + send(gamma, Y)
    late_code = send(late_go, Y)
    (early_stay,) = partial_rows(Z_FIRST, [Y, 0], 0, *rest)
    (late_stay,) = partial_rows(Y_FIRST, [0, *Z], 0, *rest)

    late_own, *late_turn = turn_z(late_stay, late_code)
    late_codes = [send(x, z) for x, z in zip(late_turn, Z)]
    early_turn, early_own = turn_y(early_stay, early_codes)
    early, *early_back = finish(early_own, [send(early_turn, Y)], 3)
    early_came = [
        give_back(early_back[0], 1, 0),
        give_back(early_back[1], 1, 1),
        give_back(early_back[2], "extra", 0),
    ]
    fitted = jnp.dot(metric_inv, gamma, precision=lax.Precision.HIGHEST)
    coulomb = jnp.einsum(
        "p,rpmn->rmn", fitted, three_index.astype(jnp.float32), precision=lax.Precision.HIGHEST
    )
    late, *late_back = finish(late_own, late_codes, 4)
    late_came = [give_back(late_back[2 * k + b], 2 + k, b) for k in range(2) for b in range(2)]
    exchange = assemble(row_block, early, late, early_came + late_came)
    return (exchange, coulomb.astype(jnp.bfloat16), fitted)


def solution(mesh):
    placed = (
        P(("groups", "row"), None, None, None),
        P(("groups", "row"), None),
        P("groups"),
        P(("groups", "row"), None, None),
        P("groups", None),
        P(("groups", "row"), None, None, None),
    )
    return jax.shard_map(
        summed_rows if mesh.shape["row"] == ROWS else sent_panels,
        mesh=mesh,
        in_specs=placed,
        out_specs=(P(("groups", "row"), None, None), P(("groups", "row"), None, None), P("groups")),
        check_vma=False,
    )
```

```python
import functools
import jax
import jax.numpy as jnp
from jax import lax
from jax.experimental import pallas as pl
from jax.experimental.pallas import tpu as pltpu
from jax.sharding import PartitionSpec as P


def row_terms(rows_in, row_ids, owned, count):
    total_rows = rows_in.shape[0]
    group = 32
    slots = rows_in.shape[1]
    width = rows_in.shape[3]
    grouped = rows_in.reshape((total_rows // group, group) + rows_in.shape[1:])
    grouped_ids = row_ids.reshape(total_rows // group, group, slots)

    def step(total, item):
        block_rows, block_ids = item
        chosen = (block_ids == owned).astype(jnp.bfloat16)
        picked = jnp.einsum(
            "gs,gspk->gpk", chosen, block_rows, preferred_element_type=jnp.float32
        ).astype(jnp.bfloat16)
        prods = jnp.einsum("gpk,gspn->gskn", picked, block_rows, preferred_element_type=jnp.float32)
        target = jnp.maximum(block_ids, 0).reshape(-1)
        added = jax.ops.segment_sum(prods.reshape(-1, width, width), target, num_segments=count)
        return (total + added, None)

    start = jnp.zeros((count, width, width), jnp.float32)
    total, _ = lax.scan(step, start, (grouped, grouped_ids))
    return total


def sent_panels(panels, blocks, row_block, coeffs, metric_inv, three_index):
    count = row_block.shape[0]
    orbits, slots, aux, width = panels.shape
    capacity = max(2, (orbits * slots + count - 1) // count)
    here = lax.axis_index("row")
    owned = row_block[here]
    ranks = jnp.arange(count, dtype=jnp.int32)
    flat_ids = blocks.reshape(-1)
    matches = (row_block[None, :] == flat_ids[:, None]).astype(jnp.int32)
    target = jnp.sum(matches * ranks[None, :], axis=1)
    hits = (ranks[None, :] == target[:, None]).astype(jnp.int32)
    before = jnp.cumsum(hits, axis=0) - hits
    place = jnp.sum(before * hits, axis=1)
    source = jnp.repeat(panels, slots, axis=0)
    source_ids = jnp.repeat(blocks, slots, axis=0).astype(jnp.bfloat16)
    outgoing = (
        jnp.zeros((count, capacity, slots, aux, width), jnp.bfloat16).at[target, place].set(source)
    )
    outgoing_ids = (
        jnp.full((count, capacity, slots), -1.0, jnp.bfloat16).at[target, place].set(source_ids)
    )
    partial_terms = jnp.einsum(
        "ispm,ism->p", panels.astype(jnp.float32), coeffs, precision=lax.Precision.HIGHEST
    )
    gamma = lax.psum(partial_terms, "row")
    fitted = jnp.dot(metric_inv, gamma, precision=lax.Precision.HIGHEST)
    coulomb = jnp.einsum(
        "p,rpmn->rmn", fitted, three_index.astype(jnp.float32), precision=lax.Precision.HIGHEST
    )
    arrived, arrived_ids = (
        lax.all_to_all(outgoing, "row", split_axis=0, concat_axis=0, tiled=True),
        lax.all_to_all(outgoing_ids, "row", split_axis=0, concat_axis=0, tiled=True),
    )
    accum = row_terms(
        arrived.reshape(-1, slots, aux, width),
        arrived_ids.reshape(-1, slots).astype(jnp.int32),
        owned,
        count,
    )
    exchange = accum.transpose(1, 0, 2).reshape(width, count * width)[None].astype(jnp.bfloat16)
    return (exchange, coulomb.astype(jnp.bfloat16), fitted)


ROWS = 16
CORE, Y, Z = 1, 2, (4, 8, 12)
PLACES = 16
Z_FIRST, Y_FIRST = (3, "extra"), (1, 2, 0)
TAIL = 16
TOP = 14.99
VECTOR = 8
AHEAD = 6
SHORT = pl.CostEstimate(flops=1024, bytes_accessed=1024, transcendentals=0)


def send(x, flip):
    return lax.ppermute(x, "row", [(i, i ^ flip) for i in range(ROWS)])


def swap_low(index):
    return (index & 12) | ((index & 1) << 1) | ((index >> 1) & 1)


def side_of(z, apart):
    return (z >> 1) & 1 if apart == 2 else z & 1


def first_place(row, region):
    if region == 0:
        return 0
    if region == "extra":
        return 2 + (row & 1)
    return region * 4 + side_of(row >> 2, region) * 2


def width_of(region):
    return 1 if region == "extra" else 2


def encode(out, sums, vector=()):
    height, columns = sums[0].shape
    line = lax.broadcasted_iota(jnp.int32, (TAIL, columns), 0)
    tail = jnp.zeros((TAIL, columns), jnp.float32)
    for j, x in enumerate(sums):
        peak = jnp.maximum(jnp.max(jnp.abs(x), axis=0, keepdims=True), 2.0**-100)
        exponent = jnp.ceil(jnp.log2(peak) * 8)
        scaled = jnp.round(x * jnp.exp2(TOP - exponent * 0.125))
        out[j * height : (j + 1) * height, :] = scaled.astype(jnp.int32).astype(jnp.int16)
        tail = jnp.where(line == j, exponent, tail)
    for j, x in enumerate(vector):
        rest = jnp.zeros((1, columns - x.shape[1]), jnp.float32)
        tail = jnp.where(line == VECTOR + j, jnp.concatenate([x, rest], axis=1), tail)
    out[len(sums) * height :, :] = tail.astype(jnp.int32).astype(jnp.int16)


def encode_vector(x):
    exponent = jnp.ceil(jnp.log2(jnp.maximum(jnp.abs(x), 2.0**-100)))
    scaled = x * jnp.exp2(14 - exponent)
    high = jnp.round(scaled)
    low = jnp.round((scaled - high) * 2.0**15)
    return (exponent, high, low), combine(exponent, high, low)


def combine(exponent, high, low):
    return (high + low * 2.0**-15) * jnp.exp2(exponent - 14)


def decode_vector(codes, width):
    tail = codes[codes.shape[0] - TAIL :, :width].astype(jnp.int32).astype(jnp.float32)
    return combine(*(tail[VECTOR + j : VECTOR + j + 1, :] for j in range(3)))


def decode(codes, j, height):
    count = (codes.shape[0] - TAIL) // height
    exponents = codes[count * height :, :].astype(jnp.int32).astype(jnp.float32)
    scale = jnp.exp2(exponents[j : j + 1, :] * 0.125 - TOP)
    return codes[j * height : (j + 1) * height, :].astype(jnp.int32).astype(jnp.float32) * scale


def rows_kernel(jobs, project, listed, ranks, listed_other, ranks_other, mine, other_far, *refs):
    if project:
        coeffs, refs = refs[0], refs[1:]
    outs, (other, arrived), picks, spreads = refs[: -2 * AHEAD - 2], refs[-2:], refs[-2 * AHEAD - 2 : -AHEAD - 2], refs[-AHEAD - 2 : -2]
    orbits, slots, aux, width = mine.shape
    capacity = listed.shape[1]
    me = lax.axis_index("row")
    copy = pltpu.make_async_copy(other_far, other, arrived)
    copy.start()
    todo = [(job, j) for job in range(len(jobs)) for j in range(len(jobs[job][1]))]

    def spans_of(job, j):
        group, flips, _ = jobs[job]
        return [
            pl.ds(pl.multiple_of(first_place(me ^ flips[j], region) * width, width), width_of(region) * width)
            for region in group
        ]

    def gather(step, side):
        job, j = todo[step]
        row = me ^ jobs[job][1][j]
        row_rank = swap_low(row)
        picked, spread = picks[step % AHEAD], spreads[step % AHEAD]
        names, places_of, panels = ((listed, ranks, mine), (listed_other, ranks_other, other))[side]
        half = capacity * aux
        for span in spans_of(job, j):
            spread[side * half : (side + 1) * half, span] = jnp.zeros((half, span.size), jnp.bfloat16)
        for n in range(capacity):
            code = names[row, n]
            orbit, slot = jnp.maximum(code, 0) >> 3, jnp.maximum(code, 0) & 7
            at = pl.ds((side * capacity + n) * aux, aux)
            chosen = panels[orbit, slot]
            tiles = [panels[orbit, t] for t in range(slots)]
            places = [places_of[orbit, t] ^ row_rank for t in range(slots)]
            picked[at, :] = jnp.where(code >= 0, chosen, jnp.zeros_like(chosen))
            for tile, place in zip(tiles, places):
                spread[at, pl.ds(pl.multiple_of(place * width, width), width)] = tile

    for step in range(min(AHEAD, len(todo))):
        gather(step, 0)
    vector = ()
    if project:
        total = jnp.zeros((aux, width), jnp.float32)
        for i in range(orbits):
            for t in range(slots):
                total = total + mine[i, t].astype(jnp.float32) * coeffs[i, t : t + 1, :]
        total = jnp.sum(total.T, axis=0, keepdims=True)
        total = jnp.concatenate([total, jnp.zeros((1, width - aux), jnp.float32)], axis=1)
        vector, kept = encode_vector(total)
        outs[-1][...] = jnp.broadcast_to(kept, outs[-1].shape)
    copy.wait()
    first, gathered = 0, []
    for step, (job, j) in enumerate(todo):
        gather(step, 1)
        picked, spread = picks[step % AHEAD], spreads[step % AHEAD]
        sums = [
            lax.dot_general(
                picked[...],
                spread[:, span],
                (((0,), (0,)), ((), ())),
                preferred_element_type=jnp.float32,
            )
            for span in spans_of(job, j)
        ]
        if step + AHEAD < len(todo):
            gather(step + AHEAD, 0)
        group, flips, per_message = jobs[job]
        if per_message:
            gathered.append(jnp.concatenate(sums, axis=1))
            if len(gathered) == per_message:
                encode(outs[first], gathered, vector if job + 1 == len(jobs) else ())
                first, gathered = first + 1, []
        else:
            at = 0
            for x in sums:
                outs[first][j, :, at : at + x.shape[1]] = x
                at += x.shape[1]
            first += j + 1 == len(flips)


def partial_rows(jobs, lists, ranks, panels, *coeffs):
    orbits, slots, aux, width = panels[0].shape
    depth = 2 * lists[0].shape[1] * aux
    shapes = []
    for group, flips, per_message in jobs:
        columns = sum(width_of(region) for region in group) * width
        if per_message:
            message = jax.ShapeDtypeStruct((per_message * width + TAIL, columns), jnp.int16)
            shapes += [message] * (len(flips) // per_message)
        else:
            shapes.append(jax.ShapeDtypeStruct((len(flips), width, columns), jnp.float32))
    if coeffs:
        shapes.append(jax.ShapeDtypeStruct((8, width), jnp.float32))
    scalars = pl.BlockSpec(memory_space=pltpu.SMEM)
    whole = pl.BlockSpec(memory_space=pltpu.VMEM)
    return pl.pallas_call(
        functools.partial(rows_kernel, jobs, len(coeffs)),
        in_specs=[scalars] * 4 + [whole, pl.BlockSpec(memory_space=pl.ANY)] + [whole] * len(coeffs),
        out_specs=[whole] * len(shapes),
        out_shape=shapes,
        scratch_shapes=[pltpu.VMEM((depth, width), jnp.bfloat16)] * AHEAD
        + [pltpu.VMEM((depth, PLACES * width), jnp.bfloat16)] * AHEAD
        + [pltpu.VMEM(panels[1].shape, jnp.bfloat16), pltpu.SemaphoreType.DMA],
        compiler_params=pltpu.CompilerParams(vmem_limit_bytes=40 << 20),
        cost_estimate=SHORT,
    )(lists[0], ranks[0], lists[1], ranks[1], *panels, *coeffs)


def turn_kernel(late_stay, late_code, early_stay, vector, *refs):
    codes, (late_own, *late_turn), (early_own, early_turn, vector_out) = refs[:3], refs[3:7], refs[7:]
    height = late_own.shape[0]
    for j, out in enumerate(late_turn):
        encode(out, [late_stay[j + 1] + decode(late_code, j + 1, height)])
    near, far, across = [decode_vector(c, vector.shape[1]) for c in codes]
    rows, kept = encode_vector((vector[0:1, :] + near) + (far + across))
    vector_out[...] = jnp.broadcast_to(kept, vector_out.shape)
    encode(early_turn, [early_stay[0] + sum(decode(c, 0, height) for c in codes)], rows)
    late_own[...] = late_stay[0] + decode(late_code, 0, height)
    early_own[...] = early_stay[1] + sum(decode(c, 1, height) for c in codes)


def turn(late_stay, late_code, early_stay, vector, early_codes):
    def shapes(stay):
        height, columns = stay.shape[1:]
        message = jax.ShapeDtypeStruct((height + TAIL, columns), jnp.int16)
        return jax.ShapeDtypeStruct((height, columns), jnp.float32), message

    late_own, late_turn = shapes(late_stay)
    return pl.pallas_call(
        turn_kernel,
        out_shape=[late_own] + [late_turn] * 3 + [*shapes(early_stay), vector],
        compiler_params=pltpu.CompilerParams(vmem_limit_bytes=32 << 20),
        cost_estimate=SHORT,
    )(late_stay, late_code, early_stay, vector, *early_codes)


def coulomb_kernel(vector, vector_other, metric, tiles, fitted, out):
    aux, height, width = tiles.shape[1:]
    gamma = (vector[...] + vector_other[...])[0:1, :aux]
    column = jnp.sum(metric[...] * gamma, axis=1, keepdims=True)
    fitted[...] = jnp.broadcast_to(column, (aux, width)).T[0:1, :]
    total = jnp.zeros((height, width), jnp.float32)
    for p in range(aux):
        total = total + column[p : p + 1, 0:1] * tiles[0, p].astype(jnp.float32)
    out[0] = total.astype(jnp.bfloat16)


def coulomb_tile(vector, vector_other, metric_inv, three_index):
    aux, height, width = three_index.shape[1:]
    return pl.pallas_call(
        coulomb_kernel,
        out_shape=[
            jax.ShapeDtypeStruct((1, aux), jnp.float32),
            jax.ShapeDtypeStruct((1, height, width), jnp.bfloat16),
        ],
        compiler_params=pltpu.CompilerParams(vmem_limit_bytes=32 << 20),
        cost_estimate=SHORT,
    )(vector, vector_other, metric_inv, three_index)


def finish_kernel(backs, own, *refs):
    codes, done, back = refs[: -backs - 1], refs[-backs - 1], refs[len(refs) - backs :]
    height = own.shape[0]
    total = own[...] + sum(decode(c, 0, height) for c in codes)
    done[...] = total.astype(jnp.bfloat16)
    for b, out in enumerate(back):
        out[...] = total[:, b * height : (b + 1) * height].T.astype(jnp.bfloat16)


def finish(own, codes, backs):
    height, columns = own.shape
    return pl.pallas_call(
        functools.partial(finish_kernel, backs),
        out_shape=[jax.ShapeDtypeStruct((height, columns), jnp.bfloat16)]
        + [jax.ShapeDtypeStruct((height, height), jnp.bfloat16)] * backs,
        compiler_params=pltpu.CompilerParams(vmem_limit_bytes=32 << 20),
        cost_estimate=SHORT,
    )(own, *codes)


def finish_early_kernel(own, code, vector, *refs):
    finish_kernel(len(refs) - 2, own, code, *refs[:-1])
    refs[-1][...] = vector[...] + decode_vector(code, vector.shape[1])


def finish_early(own, code, vector):
    height, columns = own.shape
    backs = columns // height
    return pl.pallas_call(
        finish_early_kernel,
        out_shape=[jax.ShapeDtypeStruct((height, columns), jnp.bfloat16)]
        + [jax.ShapeDtypeStruct((height, height), jnp.bfloat16)] * backs
        + [jax.ShapeDtypeStruct(vector.shape, jnp.float32)],
        compiler_params=pltpu.CompilerParams(vmem_limit_bytes=32 << 20),
        cost_estimate=SHORT,
    )(own, code, vector)


def give_back(block, region, b):
    def holder(i):
        return i ^ swap_low(first_place(i, region) + b)

    return lax.ppermute(block, "row", [(i, holder(i)) for i in range(ROWS)])


def return_blocks(finished, group):
    row, *back = finished
    named = [(region, b) for region in group if region != 0 for b in range(width_of(region))]
    return row, [give_back(block, *name) for block, name in zip(back, named)]


def assemble_kernel(holders, early, late, *refs):
    came, out = refs[:-1], refs[-1]
    width = early.shape[0]
    me = lax.axis_index("row")
    rank = swap_low(me)

    def put(place, block):
        column = holders[swap_low(place ^ rank)]
        out[0, :, pl.ds(pl.multiple_of(column * width, width), width)] = block

    k = 0
    for group, rows in ((Z_FIRST, early), (Y_FIRST, late)):
        at = 0
        for region in group:
            start = first_place(me, region)
            for b in range(width_of(region)):
                put(start + b, rows[:, at * width : (at + 1) * width])
                at += 1
                if region == 0:
                    continue
                other = 5 - start if region == "extra" else region * 8 + 2 - start + b
                put(other, came[k][...])
                k += 1


def assemble(row_block, early, late, came):
    width = early.shape[0]
    vmem = pl.BlockSpec(memory_space=pltpu.VMEM)
    return pl.pallas_call(
        assemble_kernel,
        in_specs=[pl.BlockSpec(memory_space=pltpu.SMEM)] + [vmem] * (2 + len(came)),
        out_shape=jax.ShapeDtypeStruct((1, width, ROWS * width), jnp.bfloat16),
        cost_estimate=SHORT,
    )(row_block, early, late, *came)


def naming(blocks, row_block, capacity):
    orbits, slots = blocks.shape
    holders = jnp.arange(ROWS, dtype=jnp.int32)
    hits = (blocks[:, :, None] == row_block[None, None, :]).astype(jnp.int32)
    rank = jnp.sum(hits * swap_low(holders), axis=2)
    named = jnp.sum(hits, axis=1)
    code = jnp.arange(orbits, dtype=jnp.int32)[:, None] * 8 + jnp.sum(
        hits * jnp.arange(slots, dtype=jnp.int32)[None, :, None], axis=1
    )
    earlier = (jnp.arange(orbits)[None, :] < jnp.arange(orbits)[:, None]).astype(jnp.int32)
    before = jnp.sum(earlier[:, :, None] * named[None, :, :], axis=1)
    here = (before[:, :, None] == jnp.arange(capacity)) & (named[:, :, None] > 0)
    listed = jnp.sum(jnp.where(here, code[:, :, None] + 1, 0), axis=0) - 1
    return listed, rank


def summed_rows(panels, blocks, row_block, coeffs, metric_inv, three_index):
    orbits, slots, aux, width = panels.shape
    capacity = orbits * slots // ROWS

    other = send(panels, CORE)
    listed, rank = naming(blocks, row_block, capacity)
    listed_other, rank_other = send(listed, CORE), send(rank, CORE)
    ranks, sides = (rank, rank_other), (panels, other)

    jobs = (Y_FIRST, [Y] + [z | Y for z in Z], 4), (Z_FIRST, [z | y for z in Z for y in (Y, 0)], 2)
    late_go, *early_go, vector = partial_rows(jobs, (listed, listed_other), ranks, sides, coeffs)
    across, far = send(early_go[2], Z[2]), send(early_go[1], Z[1])
    late_code = send(late_go, Y)
    early_codes = [send(early_go[0], Z[0]), far, across]

    listed, *_ = lax.optimization_barrier((listed, late_go, *early_go))
    jobs = (Y_FIRST, [0, *Z], 0), (Z_FIRST, [Y, 0], 0)
    late_stay, early_stay = partial_rows(jobs, (listed, listed_other), ranks, sides)

    late_own, *late_turn, early_own, early_turn, vector = turn(
        late_stay, late_code, early_stay, vector, early_codes
    )
    across, far = send(late_turn[2], Z[2]), send(late_turn[1], Z[1])
    late_codes = [send(late_turn[0], Z[0]), far, across]
    *early_out, vector = finish_early(early_own, send(early_turn, Y), vector)
    early, early_came = return_blocks(early_out, Z_FIRST)
    fitted, coulomb = coulomb_tile(vector, send(vector, CORE), metric_inv, three_index)
    late, late_came = return_blocks(finish(late_own, late_codes, 4), Y_FIRST)
    exchange = assemble(row_block, early, late, early_came + late_came)
    return (exchange, coulomb, fitted[0])


def solution(mesh):
    placed = (
        P(("groups", "row"), None, None, None),
        P(("groups", "row"), None),
        P("groups"),
        P(("groups", "row"), None, None),
        P("groups", None),
        P(("groups", "row"), None, None, None),
    )
    return jax.shard_map(
        summed_rows if mesh.shape["row"] == ROWS else sent_panels,
        mesh=mesh,
        in_specs=placed,
        out_specs=(P(("groups", "row"), None, None), P(("groups", "row"), None, None), P("groups")),
        check_vma=False,
    )
```

```python
import functools
import jax
import jax.numpy as jnp
from jax import lax
from jax.experimental import pallas as pl
from jax.experimental.pallas import tpu as pltpu
from jax.sharding import PartitionSpec as P


def row_terms(rows_in, row_ids, owned, count):
    total_rows = rows_in.shape[0]
    group = 32
    slots = rows_in.shape[1]
    width = rows_in.shape[3]
    grouped = rows_in.reshape((total_rows // group, group) + rows_in.shape[1:])
    grouped_ids = row_ids.reshape(total_rows // group, group, slots)

    def step(total, item):
        block_rows, block_ids = item
        chosen = (block_ids == owned).astype(jnp.bfloat16)
        picked = jnp.einsum(
            "gs,gspk->gpk", chosen, block_rows, preferred_element_type=jnp.float32
        ).astype(jnp.bfloat16)
        prods = jnp.einsum("gpk,gspn->gskn", picked, block_rows, preferred_element_type=jnp.float32)
        target = jnp.maximum(block_ids, 0).reshape(-1)
        added = jax.ops.segment_sum(prods.reshape(-1, width, width), target, num_segments=count)
        return (total + added, None)

    start = jnp.zeros((count, width, width), jnp.float32)
    total, _ = lax.scan(step, start, (grouped, grouped_ids))
    return total


def sent_panels(panels, blocks, row_block, coeffs, metric_inv, three_index):
    count = row_block.shape[0]
    orbits, slots, aux, width = panels.shape
    capacity = max(2, (orbits * slots + count - 1) // count)
    here = lax.axis_index("row")
    owned = row_block[here]
    ranks = jnp.arange(count, dtype=jnp.int32)
    flat_ids = blocks.reshape(-1)
    matches = (row_block[None, :] == flat_ids[:, None]).astype(jnp.int32)
    target = jnp.sum(matches * ranks[None, :], axis=1)
    hits = (ranks[None, :] == target[:, None]).astype(jnp.int32)
    before = jnp.cumsum(hits, axis=0) - hits
    place = jnp.sum(before * hits, axis=1)
    source = jnp.repeat(panels, slots, axis=0)
    source_ids = jnp.repeat(blocks, slots, axis=0).astype(jnp.bfloat16)
    outgoing = (
        jnp.zeros((count, capacity, slots, aux, width), jnp.bfloat16).at[target, place].set(source)
    )
    outgoing_ids = (
        jnp.full((count, capacity, slots), -1.0, jnp.bfloat16).at[target, place].set(source_ids)
    )
    partial_terms = jnp.einsum(
        "ispm,ism->p", panels.astype(jnp.float32), coeffs, precision=lax.Precision.HIGHEST
    )
    gamma = lax.psum(partial_terms, "row")
    fitted = jnp.dot(metric_inv, gamma, precision=lax.Precision.HIGHEST)
    coulomb = jnp.einsum(
        "p,rpmn->rmn", fitted, three_index.astype(jnp.float32), precision=lax.Precision.HIGHEST
    )
    arrived, arrived_ids = (
        lax.all_to_all(outgoing, "row", split_axis=0, concat_axis=0, tiled=True),
        lax.all_to_all(outgoing_ids, "row", split_axis=0, concat_axis=0, tiled=True),
    )
    accum = row_terms(
        arrived.reshape(-1, slots, aux, width),
        arrived_ids.reshape(-1, slots).astype(jnp.int32),
        owned,
        count,
    )
    exchange = accum.transpose(1, 0, 2).reshape(width, count * width)[None].astype(jnp.bfloat16)
    return (exchange, coulomb.astype(jnp.bfloat16), fitted)


ROWS = 16
CORE, Y, Z = 1, 2, (4, 8, 12)
NEAR, FAR = 4, 12
PLACES = 16
Z_FIRST, SOONER, LATER = (3, "extra"), (1, 2), (0,)
TAIL = 8
TOP = 14.99
VECTOR = 4
AHEAD = 6
SHORT = pl.CostEstimate(flops=1024, bytes_accessed=1024, transcendentals=0)
LONG = pl.CostEstimate(flops=1 << 34, bytes_accessed=1024, transcendentals=0)


def send(x, flip):
    return lax.ppermute(x, "row", [(i, i ^ flip) for i in range(ROWS)])


def side_of(z, apart):
    return (z >> 1) & 1 if apart == 2 else z & 1


def first_place(row, region):
    if region == 0:
        return 0
    if region == "extra":
        return 2 + ((row >> 1) & 1)
    return region * 4 + side_of(row >> 2, region) * 2


def width_of(region):
    return 1 if region == "extra" else 2


def encode(out, sums, vector=()):
    height, columns = sums[0].shape
    line = lax.broadcasted_iota(jnp.int32, (TAIL, columns), 0)
    tail = jnp.zeros((TAIL, columns), jnp.float32)
    for j, x in enumerate(sums):
        peak = jnp.maximum(jnp.max(jnp.abs(x), axis=0, keepdims=True), 2.0**-100)
        exponent = jnp.ceil(jnp.log2(peak) * 8)
        scaled = jnp.round(x * jnp.exp2(TOP - exponent * 0.125))
        out[j * height : (j + 1) * height, :] = scaled.astype(jnp.int32).astype(jnp.int16)
        tail = jnp.where(line == j, exponent, tail)
    for j, x in enumerate(vector):
        rest = jnp.zeros((1, columns - x.shape[1]), jnp.float32)
        tail = jnp.where(line == VECTOR + j, jnp.concatenate([x, rest], axis=1), tail)
    out[len(sums) * height :, :] = tail.astype(jnp.int32).astype(jnp.int16)


def encode_vector(x):
    exponent = jnp.ceil(jnp.log2(jnp.maximum(jnp.abs(x), 2.0**-100)))
    scaled = x * jnp.exp2(14 - exponent)
    high = jnp.round(scaled)
    low = jnp.round((scaled - high) * 2.0**15)
    return (exponent, high, low), combine(exponent, high, low)


def combine(exponent, high, low):
    return (high + low * 2.0**-15) * jnp.exp2(exponent - 14)


def decode_vector(codes, width):
    tail = codes[codes.shape[0] - TAIL :, :width].astype(jnp.int32).astype(jnp.float32)
    return combine(*(tail[VECTOR + j : VECTOR + j + 1, :] for j in range(3)))


def decode(codes, j, height):
    count = (codes.shape[0] - TAIL) // height
    exponents = codes[count * height :, :].astype(jnp.int32).astype(jnp.float32)
    scale = jnp.exp2(exponents[j : j + 1, :] * 0.125 - TOP)
    return codes[j * height : (j + 1) * height, :].astype(jnp.int32).astype(jnp.float32) * scale


def bring_kernel(far, near, arrived):
    copy = pltpu.make_async_copy(far, near, arrived)
    copy.start()
    copy.wait()


def bring(panels):
    return pl.pallas_call(
        bring_kernel,
        in_specs=[pl.BlockSpec(memory_space=pltpu.HBM)],
        out_specs=pl.BlockSpec(memory_space=pltpu.VMEM),
        out_shape=jax.ShapeDtypeStruct(panels.shape, panels.dtype),
        scratch_shapes=[pltpu.SemaphoreType.DMA],
        compiler_params=pltpu.CompilerParams(vmem_limit_bytes=16 << 20),
        cost_estimate=SHORT,
    )(panels)


def density_of(panels, coeffs):
    orbits, slots, aux, width = panels.shape
    total = jnp.zeros((aux, width), jnp.float32)
    for i in range(orbits):
        for t in range(slots):
            total = total + panels[i, t].astype(jnp.float32) * coeffs[t, i : i + 1, :]
    return total


def rows_kernel(jobs, project, listed, ranks, listed_other, ranks_other, mine, other_far, *refs):
    if project:
        coeffs, coeffs_other, refs = refs[0], refs[1], refs[2:]
    outs, (other, arrived), picks, spreads = refs[: -2 * AHEAD - 2], refs[-2:], refs[-2 * AHEAD - 2 : -AHEAD - 2], refs[-AHEAD - 2 : -2]
    orbits, slots, aux, width = mine.shape
    capacity = listed.shape[1]
    me = lax.axis_index("row")
    copy = pltpu.make_async_copy(other_far, other, arrived)
    copy.start()
    todo = [(job, j) for job in range(len(jobs)) for j in range(len(jobs[job][1]))]

    def spans_of(job, j):
        groups, flips, _ = jobs[job]
        return [
            [
                pl.ds(pl.multiple_of(first_place(me ^ flips[j], region) * width, width), width_of(region) * width)
                for region in group
            ]
            for group in groups
        ]

    def gather(step, side):
        job, j = todo[step]
        row = me ^ jobs[job][1][j]
        picked, spread = picks[step % AHEAD], spreads[step % AHEAD]
        names, places_of, panels = ((listed, ranks, mine), (listed_other, ranks_other, other))[side]
        half = capacity * aux
        for span in sum(spans_of(job, j), []):
            spread[side * half : (side + 1) * half, span] = jnp.zeros((half, span.size), jnp.bfloat16)
        for n in range(capacity):
            code = names[row, n]
            orbit, slot = jnp.maximum(code, 0) >> 3, jnp.maximum(code, 0) & 7
            at = pl.ds((side * capacity + n) * aux, aux)
            chosen = panels[orbit, slot]
            tiles = [panels[orbit, t] for t in range(slots)]
            places = [places_of[t, orbit] ^ row for t in range(slots)]
            picked[at, :] = jnp.where(code >= 0, chosen, jnp.zeros_like(chosen))
            for tile, place in zip(tiles, places):
                spread[at, pl.ds(pl.multiple_of(place * width, width), width)] = tile

    for step in range(min(AHEAD, len(todo))):
        gather(step, 0)
    if project:
        total = density_of(mine, coeffs)
    copy.wait()
    vector = ()
    if project:
        total = jnp.sum((total + density_of(other, coeffs_other)).T, axis=0, keepdims=True)
        total = jnp.concatenate([total, jnp.zeros((1, width - aux), jnp.float32)], axis=1)
        vector, outs[-1][...] = encode_vector(total)
    first, gathered = 0, {}
    for step, (job, j) in enumerate(todo):
        gather(step, 1)
        picked, spread = picks[step % AHEAD], spreads[step % AHEAD]
        sums = [
            [
                lax.dot_general(
                    picked[...],
                    spread[:, span],
                    (((0,), (0,)), ((), ())),
                    preferred_element_type=jnp.float32,
                )
                for span in spans
            ]
            for spans in spans_of(job, j)
        ]
        if step + AHEAD < len(todo):
            gather(step + AHEAD, 0)
        groups, flips, coded = jobs[job]
        for k, parts in enumerate(sums):
            out = outs[first + k]
            row = jnp.concatenate(parts, axis=1) if len(parts) > 1 else parts[0]
            if not coded:
                out[j] = row
                continue
            gathered.setdefault((job, k), []).append(row)
            if j + 1 == len(flips):
                encode(out, gathered[job, k], vector if job + 1 == len(jobs) else ())
        if j + 1 == len(flips):
            first += len(groups)


def partial_rows(jobs, lists, ranks, panels, *coeffs):
    orbits, slots, aux, width = panels[0].shape
    depth = 2 * lists[0].shape[1] * aux
    shapes = []
    for groups, flips, coded in jobs:
        for group in groups:
            columns = sum(width_of(region) for region in group) * width
            if coded:
                shapes.append(message_of(len(flips) * width, columns))
            else:
                shapes.append(sums_of(len(flips), width, columns))
    if coeffs:
        shapes.append(jax.ShapeDtypeStruct((1, width), jnp.float32))
    scalars = pl.BlockSpec(memory_space=pltpu.SMEM)
    whole = pl.BlockSpec(memory_space=pltpu.VMEM)
    return pl.pallas_call(
        functools.partial(rows_kernel, jobs, len(coeffs)),
        in_specs=[scalars] * 4 + [whole, pl.BlockSpec(memory_space=pltpu.HBM)] + [whole] * len(coeffs),
        out_specs=[whole] * len(shapes),
        out_shape=shapes,
        scratch_shapes=[pltpu.VMEM((depth, width), jnp.bfloat16)] * AHEAD
        + [pltpu.VMEM((depth, PLACES * width), jnp.bfloat16)] * AHEAD
        + [pltpu.VMEM(panels[1].shape, jnp.bfloat16), pltpu.SemaphoreType.DMA],
        compiler_params=pltpu.CompilerParams(vmem_limit_bytes=28 << 20),
        cost_estimate=SHORT if coeffs else LONG,
    )(lists[0], ranks[0], lists[1], ranks[1], *panels, *coeffs)


def turn_y_kernel(stay, code, kept, message):
    height = stay.shape[1]
    encode(message, [stay[j] + decode(code, j, height) for j in (1, 2)])
    for k, j in enumerate((0, 3)):
        kept[k] = stay[j] + decode(code, j, height)


def turn_z_kernel(kept, code, own, message):
    height = own.shape[0]
    encode(message, [kept[1] + decode(code, 1, height)])
    own[...] = kept[0] + decode(code, 0, height)


def turn_near_kernel(stay, projected, code, kept, message, vector):
    height = kept.shape[1]
    rows, vector[...] = encode_vector(projected[...] + decode_vector(code, projected.shape[1]))
    encode(message, [stay[j] + decode(code, j, height) for j in (2, 3)], rows)
    for j in range(2):
        kept[j] = stay[j] + decode(code, j, height)


def turn_far_kernel(stay, projected, code, own, message, vector, extra):
    height, width = own.shape[0], extra.shape[1]
    rows, vector[...] = encode_vector(projected[...] + decode_vector(code, projected.shape[1]))
    theirs, mine = [stay[j] + decode(code, j, height) for j in range(2)]
    encode(message, [jnp.concatenate([theirs, mine[:, -width:]], axis=1)], rows)
    own[...] = mine
    extra[...] = theirs[:, -width:]


def message_of(rows, columns):
    return jax.ShapeDtypeStruct((rows + TAIL, columns), jnp.int16)


def small_call(kernel, shapes, *args):
    return pl.pallas_call(
        kernel,
        out_shape=shapes,
        compiler_params=pltpu.CompilerParams(vmem_limit_bytes=16 << 20),
        cost_estimate=SHORT,
    )(*args)


def sums_of(*shape):
    return jax.ShapeDtypeStruct(shape, jnp.float32)


def turn_y(stay, code):
    height, columns = stay.shape[1:]
    shapes = [sums_of(2, height, columns), message_of(2 * height, columns)]
    return small_call(turn_y_kernel, shapes, stay, code)


def turn_z(kept, code):
    height, columns = kept.shape[1:]
    shapes = [sums_of(height, columns), message_of(height, columns)]
    return small_call(turn_z_kernel, shapes, kept, code)


def turn_near(stay, projected, code):
    height, columns = stay.shape[1:]
    shapes = [sums_of(2, height, columns), message_of(2 * height, columns), sums_of(1, projected.shape[1])]
    return small_call(turn_near_kernel, shapes, stay, projected, code)


def turn_far(stay, projected, code):
    height, columns = stay.shape[1:]
    shapes = [sums_of(height, columns), message_of(height, columns + height), sums_of(*projected.shape)]
    shapes.append(sums_of(height, height))
    return small_call(turn_far_kernel, shapes, stay, projected, code)


def coulomb_kernel(vector, metric, tiles, fitted, out):
    aux, height, width = tiles.shape[1:]
    column = jnp.sum(metric[...] * vector[0:1, :aux], axis=1, keepdims=True)
    fitted[...] = jnp.broadcast_to(column, (aux, width)).T[0:1, :]
    total = jnp.zeros((height, width), jnp.float32)
    for p in range(aux):
        total = total + column[p : p + 1, 0:1] * tiles[0, p].astype(jnp.float32)
    out[0] = total.astype(jnp.bfloat16)


def coulomb_tile(vector, metric_inv, three_index):
    aux, height, width = three_index.shape[1:]
    return pl.pallas_call(
        coulomb_kernel,
        out_shape=[
            jax.ShapeDtypeStruct((1, aux), jnp.float32),
            jax.ShapeDtypeStruct((1, height, width), jnp.bfloat16),
        ],
        compiler_params=pltpu.CompilerParams(vmem_limit_bytes=16 << 20),
        cost_estimate=SHORT,
    )(vector, metric_inv, three_index)


def finish_row(total, done, *backs):
    height = total.shape[0]
    done[...] = total.astype(jnp.bfloat16)
    for k, out in enumerate(backs):
        for b in range(2):
            at = (2 * k + b) * height
            out[b] = total[:, at : at + height].T.astype(jnp.bfloat16)


def blocks_of(count, height):
    return jax.ShapeDtypeStruct((count, height, height), jnp.bfloat16)


def finish_early_kernel(own, vector, extra, code, done, back, other_extra, vector_out):
    height, columns = own.shape
    came = decode(code, 0, height)
    finish_row(own[...] + came[:, :columns], done, back)
    other_extra[...] = (extra[...] + came[:, columns:]).T.astype(jnp.bfloat16)
    vector_out[...] = vector[...] + decode_vector(code, vector.shape[1])


def finish_early(own, vector, extra, code):
    height = own.shape[0]
    shapes = [jax.ShapeDtypeStruct(own.shape, jnp.bfloat16), blocks_of(2, height)]
    shapes += [jax.ShapeDtypeStruct((height, height), jnp.bfloat16), sums_of(*vector.shape)]
    return small_call(finish_early_kernel, shapes, own, vector, extra, code)


def finish_late_kernel(own, code, done, *backs):
    finish_row(own[...] + decode(code, 0, own.shape[0]), done, *backs)


def finish_late(own, code):
    backs = [blocks_of(2, own.shape[0])] * len(SOONER)
    return small_call(finish_late_kernel, [jax.ShapeDtypeStruct(own.shape, jnp.bfloat16)] + backs, own, code)


def give_back(blocks, region):
    came = lax.ppermute(blocks, "row", [(i, i ^ first_place(i, region)) for i in range(ROWS)])
    return came, send(came, CORE)


def assemble_kernel(holders, early, late, later, code, extra, extra_core, *refs):
    came, out = refs[:-1], refs[-1]
    width = early.shape[0]
    me = lax.axis_index("row")

    def put(place, block):
        where = pl.ds(pl.multiple_of(holders[place ^ me] * width, width), width)
        out[0, :, where] = block

    base = (later[...] + decode(code, 0, width)).astype(jnp.bfloat16)
    for group, rows in ((Z_FIRST, early), (SOONER, late), (LATER, base)):
        at = 0
        for region in group:
            start = first_place(me, region)
            for b in range(width_of(region)):
                put(start + b, rows[:, at * width : (at + 1) * width])
                at += 1
    put(5 - first_place(me, "extra"), jnp.where((me >> 1) & 1 == 0, extra_core[...], extra[...]))
    for k, region in enumerate((Z_FIRST[0], *SOONER)):
        start = region * 8 + 2 - first_place(me, region)
        put(start, came[2 * k][0])
        put(start + 1, came[2 * k + 1][1])


def assemble(row_block, early, *rest):
    width = early.shape[0]
    vmem = pl.BlockSpec(memory_space=pltpu.VMEM)
    return pl.pallas_call(
        assemble_kernel,
        in_specs=[pl.BlockSpec(memory_space=pltpu.SMEM)] + [vmem] * (1 + len(rest)),
        out_shape=jax.ShapeDtypeStruct((1, width, ROWS * width), jnp.bfloat16),
        compiler_params=pltpu.CompilerParams(vmem_limit_bytes=16 << 20),
        cost_estimate=SHORT,
    )(row_block, early, *rest)


def naming(blocks, row_block, capacity):
    slots, orbits = blocks.shape
    holders = jnp.arange(ROWS, dtype=jnp.int32)
    hits = (blocks[:, :, None] == row_block[None, None, :]).astype(jnp.int32)
    rank = jnp.sum(hits * holders, axis=2)
    named = jnp.sum(hits, axis=0)
    code = jnp.arange(orbits, dtype=jnp.int32)[:, None] * 8 + jnp.sum(
        hits * jnp.arange(slots, dtype=jnp.int32)[:, None, None], axis=0
    )
    earlier = (jnp.arange(orbits)[None, :] < jnp.arange(orbits)[:, None]).astype(jnp.int32)
    before = jnp.sum(earlier[:, :, None] * named[None, :, :], axis=1)
    here = (before[:, :, None] == jnp.arange(capacity)) & (named[:, :, None] > 0)
    listed = jnp.sum(jnp.where(here, code[:, :, None] + 1, 0), axis=0) - 1
    return listed, rank


def summed_rows(panels, blocks, row_block, coeffs, metric_inv, three_index):
    orbits, slots, aux, width = panels.shape
    capacity = orbits * slots // ROWS

    other = send(panels, CORE)
    coeffs = coeffs.transpose(1, 0, 2)
    coeffs_other = send(coeffs, CORE)
    listed, rank = naming(blocks.T, row_block, capacity)
    listed_other, rank_other = send(listed, CORE), send(rank, CORE)
    listed, rank, panels = lax.optimization_barrier((listed, rank, panels))
    mine = bring(panels)
    ranks, sides = (rank, rank_other), (mine, other)

    jobs = ((SOONER, LATER), [Y] + [z | Y for z in Z], True), ((Z_FIRST,), [4 | Y, 4, 8 | Y, 8], True)
    late_go, later_go, early_go, vector = partial_rows(
        jobs, (listed, listed_other), ranks, sides, coeffs, coeffs_other
    )
    late_code = send(late_go, Y)
    early_code = send(early_go, NEAR)
    later_code = send(later_go, Y)

    listed, *_ = lax.optimization_barrier((listed, late_go, early_go, later_go))
    jobs = ((Z_FIRST,), [Y, 0, 12 | Y, 12], False), ((SOONER, LATER), [0, *Z], False)
    early_stay, late_stay, later_stay = partial_rows(jobs, (listed, listed_other), ranks, sides)

    early_stay, early_turn, vector = turn_near(early_stay, vector, early_code)
    early_code = send(early_turn, FAR)
    late, late_turn = turn_y(late_stay, late_code)
    late, late_turn = turn_z(late, send(late_turn, NEAR))
    late_code = send(late_turn, FAR)
    later, later_turn = turn_y(later_stay, later_code)
    later, later_turn = turn_z(later, send(later_turn, NEAR))
    later_code = send(later_turn, FAR)

    early_stay, *_ = lax.optimization_barrier((early_stay, late_turn))
    early_own, early_turn, vector, extra = turn_far(early_stay, vector, early_code)
    early, early_back, extra, vector = finish_early(early_own, vector, extra, send(early_turn, Y))
    came = give_back(early_back, Z_FIRST[0])
    extra_core = send(extra, CORE)
    fitted, coulomb = coulomb_tile(vector, metric_inv, three_index)

    late, *_ = lax.optimization_barrier((late, coulomb))
    late, *late_back = finish_late(late, late_code)
    for blocks, region in zip(late_back, SOONER):
        came += give_back(blocks, region)
    exchange = assemble(row_block, early, late, later, later_code, extra, extra_core, *came)
    return (exchange, coulomb, fitted[0])


def solution(mesh):
    placed = (
        P(("groups", "row"), None, None, None),
        P(("groups", "row"), None),
        P("groups"),
        P(("groups", "row"), None, None),
        P("groups", None),
        P(("groups", "row"), None, None, None),
    )
    return jax.shard_map(
        summed_rows if mesh.shape["row"] == ROWS else sent_panels,
        mesh=mesh,
        in_specs=placed,
        out_specs=(P(("groups", "row"), None, None), P(("groups", "row"), None, None), P("groups")),
        check_vma=False,
    )
```

```python
import functools
import jax
import jax.numpy as jnp
from jax import lax
from jax.experimental import pallas as pl
from jax.experimental.pallas import tpu as pltpu
from jax.sharding import PartitionSpec as P


def row_terms(rows_in, row_ids, owned, count):
    total_rows = rows_in.shape[0]
    group = 32
    slots = rows_in.shape[1]
    width = rows_in.shape[3]
    grouped = rows_in.reshape((total_rows // group, group) + rows_in.shape[1:])
    grouped_ids = row_ids.reshape(total_rows // group, group, slots)

    def step(total, item):
        block_rows, block_ids = item
        chosen = (block_ids == owned).astype(jnp.bfloat16)
        picked = jnp.einsum(
            "gs,gspk->gpk", chosen, block_rows, preferred_element_type=jnp.float32
        ).astype(jnp.bfloat16)
        prods = jnp.einsum("gpk,gspn->gskn", picked, block_rows, preferred_element_type=jnp.float32)
        target = jnp.maximum(block_ids, 0).reshape(-1)
        added = jax.ops.segment_sum(prods.reshape(-1, width, width), target, num_segments=count)
        return (total + added, None)

    start = jnp.zeros((count, width, width), jnp.float32)
    total, _ = lax.scan(step, start, (grouped, grouped_ids))
    return total


def sent_panels(panels, blocks, row_block, coeffs, metric_inv, three_index):
    count = row_block.shape[0]
    orbits, slots, aux, width = panels.shape
    capacity = max(2, (orbits * slots + count - 1) // count)
    here = lax.axis_index("row")
    owned = row_block[here]
    ranks = jnp.arange(count, dtype=jnp.int32)
    flat_ids = blocks.reshape(-1)
    matches = (row_block[None, :] == flat_ids[:, None]).astype(jnp.int32)
    target = jnp.sum(matches * ranks[None, :], axis=1)
    hits = (ranks[None, :] == target[:, None]).astype(jnp.int32)
    before = jnp.cumsum(hits, axis=0) - hits
    place = jnp.sum(before * hits, axis=1)
    source = jnp.repeat(panels, slots, axis=0)
    source_ids = jnp.repeat(blocks, slots, axis=0).astype(jnp.bfloat16)
    outgoing = (
        jnp.zeros((count, capacity, slots, aux, width), jnp.bfloat16).at[target, place].set(source)
    )
    outgoing_ids = (
        jnp.full((count, capacity, slots), -1.0, jnp.bfloat16).at[target, place].set(source_ids)
    )
    partial_terms = jnp.einsum(
        "ispm,ism->p", panels.astype(jnp.float32), coeffs, precision=lax.Precision.HIGHEST
    )
    gamma = lax.psum(partial_terms, "row")
    fitted = jnp.dot(metric_inv, gamma, precision=lax.Precision.HIGHEST)
    coulomb = jnp.einsum(
        "p,rpmn->rmn", fitted, three_index.astype(jnp.float32), precision=lax.Precision.HIGHEST
    )
    arrived, arrived_ids = (
        lax.all_to_all(outgoing, "row", split_axis=0, concat_axis=0, tiled=True),
        lax.all_to_all(outgoing_ids, "row", split_axis=0, concat_axis=0, tiled=True),
    )
    accum = row_terms(
        arrived.reshape(-1, slots, aux, width),
        arrived_ids.reshape(-1, slots).astype(jnp.int32),
        owned,
        count,
    )
    exchange = accum.transpose(1, 0, 2).reshape(width, count * width)[None].astype(jnp.bfloat16)
    return (exchange, coulomb.astype(jnp.bfloat16), fitted)


ROWS = 16
CORE, Y, Z = 1, 2, (4, 8, 12)
NEAR, FAR = 4, 12
PLACES = 16
Z_FIRST, SOONER, LATER = (3, "extra"), (1, "diagonal"), (2, "mate")
TAIL = 8
TOP = 14.99
SPARE = 0
VECTOR = 4
AHEAD = 6
SHORT = pl.CostEstimate(flops=1024, bytes_accessed=1024, transcendentals=0)
LONG = pl.CostEstimate(flops=1 << 32, bytes_accessed=1024, transcendentals=0)


def send(x, flip):
    return lax.ppermute(x, "row", [(i, i ^ flip) for i in range(ROWS)])


def side_of(z, apart):
    return (z >> 1) & 1 if apart == 2 else z & 1


def first_place(row, region):
    if region in ("diagonal", "mate"):
        return int(region == "mate")
    if region == "extra":
        return 2 + ((row >> 1) & 1)
    return region * 4 + side_of(row >> 2, region) * 2


def returned(group):
    return [region for region in group if region in (1, 2, 3)]


def spare_of(region):
    return {Z_FIRST[0]: 32, SOONER[0]: 16, LATER[0]: 0}[region]


def width_of(region):
    return 2 if region in (1, 2, 3) else 1


def encode(out, sums, vector=()):
    height, columns = sums[0].shape
    rest = out.shape[0] - len(sums) * height
    line = lax.broadcasted_iota(jnp.int32, (rest, columns), 0)
    tail = jnp.zeros((rest, columns), jnp.float32)
    for j, x in enumerate(sums):
        peak = jnp.maximum(jnp.max(jnp.abs(x), axis=0, keepdims=True), 2.0**-100)
        exponent = jnp.ceil(jnp.log2(peak) * 8)
        scaled = jnp.round(x * jnp.exp2(TOP - exponent * 0.125))
        out[j * height : (j + 1) * height, :] = scaled.astype(jnp.int32).astype(jnp.int16)
        tail = jnp.where(line == j, exponent, tail)
    for j, x in enumerate(vector):
        beside = jnp.zeros((1, columns - x.shape[1]), jnp.float32)
        tail = jnp.where(line == VECTOR + j, jnp.concatenate([x, beside], axis=1), tail)
    out[len(sums) * height :, :] = tail.astype(jnp.int32).astype(jnp.int16)


def encode_vector(x):
    exponent = jnp.ceil(jnp.log2(jnp.maximum(jnp.abs(x), 2.0**-100)))
    scaled = x * jnp.exp2(14 - exponent)
    high = jnp.round(scaled)
    low = jnp.round((scaled - high) * 2.0**15)
    return (exponent, high, low), combine(exponent, high, low)


def combine(exponent, high, low):
    return (high + low * 2.0**-15) * jnp.exp2(exponent - 14)


def decode_vector(codes, width):
    tail = codes[codes.shape[0] - TAIL :, :width].astype(jnp.int32).astype(jnp.float32)
    return combine(*(tail[VECTOR + j : VECTOR + j + 1, :] for j in range(3)))


def decode(codes, j, height):
    count = (codes.shape[0] - TAIL) // height
    exponents = codes[count * height :, :].astype(jnp.int32).astype(jnp.float32)
    scale = jnp.exp2(exponents[j : j + 1, :] * 0.125 - TOP)
    return codes[j * height : (j + 1) * height, :].astype(jnp.int32).astype(jnp.float32) * scale


def bring_kernel(far, near, arrived):
    copy = pltpu.make_async_copy(far, near, arrived)
    copy.start()
    copy.wait()


def bring(panels):
    return pl.pallas_call(
        bring_kernel,
        in_specs=[pl.BlockSpec(memory_space=pltpu.HBM)],
        out_specs=pl.BlockSpec(memory_space=pltpu.VMEM),
        out_shape=jax.ShapeDtypeStruct(panels.shape, panels.dtype),
        scratch_shapes=[pltpu.SemaphoreType.DMA],
        compiler_params=pltpu.CompilerParams(vmem_limit_bytes=16 << 20),
        cost_estimate=SHORT,
    )(panels)


def density_of(panels, coeffs):
    orbits, slots, aux, width = panels.shape
    total = jnp.zeros((aux, width), jnp.float32)
    for i in range(orbits):
        for t in range(slots):
            total = total + panels[i, t].astype(jnp.float32) * coeffs[t, i : i + 1, :]
    return total


def rows_kernel(jobs, project, listed, ranks, listed_other, ranks_other, mine, other_far, *refs):
    if project:
        coeffs, coeffs_other, refs = refs[0], refs[1], refs[2:]
    outs, (other, arrived), picks, spreads = refs[: -2 * AHEAD - 2], refs[-2:], refs[-2 * AHEAD - 2 : -AHEAD - 2], refs[-AHEAD - 2 : -2]
    orbits, slots, aux, width = mine.shape
    capacity = listed.shape[1]
    me = lax.axis_index("row")
    copy = pltpu.make_async_copy(other_far, other, arrived)
    copy.start()
    todo = [(job, j) for job in range(len(jobs)) for j in range(len(jobs[job][1]))]

    def spans_of(job, j):
        groups, flips, _ = jobs[job]
        return [
            [
                pl.ds(pl.multiple_of(first_place(me ^ flips[j], region) * width, width), width_of(region) * width)
                for region in group
            ]
            for group in groups
        ]

    def gather(step, side):
        job, j = todo[step]
        row = me ^ jobs[job][1][j]
        picked, spread = picks[step % AHEAD], spreads[step % AHEAD]
        names, places_of, panels = ((listed, ranks, mine), (listed_other, ranks_other, other))[side]
        half = capacity * aux
        for span in sum(spans_of(job, j), []):
            spread[side * half : (side + 1) * half, span] = jnp.zeros((half, span.size), jnp.bfloat16)
        for n in range(capacity):
            code = names[row, n]
            orbit, slot = jnp.maximum(code, 0) >> 3, jnp.maximum(code, 0) & 7
            at = pl.ds((side * capacity + n) * aux, aux)
            chosen = panels[orbit, slot]
            tiles = [panels[orbit, t] for t in range(slots)]
            places = [places_of[t, orbit] ^ row for t in range(slots)]
            picked[at, :] = jnp.where(code >= 0, chosen, jnp.zeros_like(chosen))
            for tile, place in zip(tiles, places):
                spread[at, pl.ds(pl.multiple_of(place * width, width), width)] = tile

    for step in range(min(AHEAD, len(todo))):
        gather(step, 0)
    if project:
        total = density_of(mine, coeffs)
    copy.wait()
    vector = ()
    if project:
        total = jnp.sum((total + density_of(other, coeffs_other)).T, axis=0, keepdims=True)
        total = jnp.concatenate([total, jnp.zeros((1, width - aux), jnp.float32)], axis=1)
        vector, outs[-1][...] = encode_vector(total)
    first, gathered = 0, {}
    for step, (job, j) in enumerate(todo):
        gather(step, 1)
        picked, spread = picks[step % AHEAD], spreads[step % AHEAD]
        sums = [
            [
                lax.dot_general(
                    picked[...],
                    spread[:, span],
                    (((0,), (0,)), ((), ())),
                    preferred_element_type=jnp.float32,
                )
                for span in spans
            ]
            for spans in spans_of(job, j)
        ]
        if step + AHEAD < len(todo):
            gather(step + AHEAD, 0)
        groups, flips, coded = jobs[job]
        for k, parts in enumerate(sums):
            out = outs[first + k]
            row = jnp.concatenate(parts, axis=1) if len(parts) > 1 else parts[0]
            if not coded:
                out[j] = row
                continue
            gathered.setdefault((job, k), []).append(row)
            if j + 1 == len(flips):
                encode(out, gathered[job, k], vector if job + 1 == len(jobs) else ())
        if j + 1 == len(flips):
            first += len(groups)


def partial_rows(jobs, lists, ranks, panels, *coeffs):
    orbits, slots, aux, width = panels[0].shape
    depth = 2 * lists[0].shape[1] * aux
    shapes = []
    for groups, flips, coded in jobs:
        for group in groups:
            columns = sum(width_of(region) for region in group) * width
            if coded:
                spare = SPARE if group == LATER else 0
                shapes.append(message_of(len(flips) * width, columns, spare))
            else:
                shapes.append(sums_of(len(flips), width, columns))
    if coeffs:
        shapes.append(jax.ShapeDtypeStruct((1, width), jnp.float32))
    scalars = pl.BlockSpec(memory_space=pltpu.SMEM)
    whole = pl.BlockSpec(memory_space=pltpu.VMEM)
    return pl.pallas_call(
        functools.partial(rows_kernel, jobs, len(coeffs)),
        in_specs=[scalars] * 4 + [whole, pl.BlockSpec(memory_space=pltpu.HBM)] + [whole] * len(coeffs),
        out_specs=[whole] * len(shapes),
        out_shape=shapes,
        scratch_shapes=[pltpu.VMEM((depth, width), jnp.bfloat16)] * AHEAD
        + [pltpu.VMEM((depth, PLACES * width), jnp.bfloat16)] * AHEAD
        + [pltpu.VMEM(panels[1].shape, jnp.bfloat16), pltpu.SemaphoreType.DMA],
        compiler_params=pltpu.CompilerParams(vmem_limit_bytes=28 << 20),
        cost_estimate=SHORT,
    )(lists[0], ranks[0], lists[1], ranks[1], *panels, *coeffs)


def turn_y_kernel(stay, code, kept, message):
    height = stay.shape[1]
    encode(message, [stay[j] + decode(code, j, height) for j in (1, 2)])
    for k, j in enumerate((0, 3)):
        kept[k] = stay[j] + decode(code, j, height)


def turn_z_kernel(kept, code, own, message):
    height = own.shape[0]
    encode(message, [kept[1] + decode(code, 1, height)])
    own[...] = kept[0] + decode(code, 0, height)


def turn_near_kernel(stay, projected, code, kept, message, vector):
    height = kept.shape[1]
    rows, vector[...] = encode_vector(projected[...] + decode_vector(code, projected.shape[1]))
    encode(message, [stay[j] + decode(code, j, height) for j in (2, 3)], rows)
    for j in range(2):
        kept[j] = stay[j] + decode(code, j, height)


def turn_far_kernel(stay, projected, code, own, message, vector, extra):
    height, width = own.shape[0], extra.shape[1]
    rows, vector[...] = encode_vector(projected[...] + decode_vector(code, projected.shape[1]))
    theirs, mine = [stay[j] + decode(code, j, height) for j in range(2)]
    encode(message, [jnp.concatenate([theirs, mine[:, -width:]], axis=1)], rows)
    own[...] = mine
    extra[...] = theirs[:, -width:]


def message_of(rows, columns, spare=0):
    return jax.ShapeDtypeStruct((rows + TAIL + spare, columns), jnp.int16)


def small_call(kernel, shapes, *args, cost=SHORT):
    return pl.pallas_call(
        kernel,
        out_shape=shapes,
        compiler_params=pltpu.CompilerParams(vmem_limit_bytes=16 << 20),
        cost_estimate=cost,
    )(*args)


def sums_of(*shape):
    return jax.ShapeDtypeStruct(shape, jnp.float32)


def turn_y(stay, code, spare):
    height, columns = stay.shape[1:]
    shapes = [sums_of(2, height, columns), message_of(2 * height, columns, spare)]
    return small_call(turn_y_kernel, shapes, stay, code)


def turn_z(kept, code, spare):
    height, columns = kept.shape[1:]
    shapes = [sums_of(height, columns), message_of(height, columns, spare)]
    return small_call(turn_z_kernel, shapes, kept, code)


def turn_near(stay, projected, code):
    height, columns = stay.shape[1:]
    shapes = [sums_of(2, height, columns), message_of(2 * height, columns), sums_of(1, projected.shape[1])]
    return small_call(turn_near_kernel, shapes, stay, projected, code)


def turn_far(stay, projected, code):
    height, columns = stay.shape[1:]
    shapes = [sums_of(height, columns), message_of(height, columns + height), sums_of(*projected.shape)]
    shapes.append(sums_of(height, height))
    return small_call(turn_far_kernel, shapes, stay, projected, code)


def coulomb_kernel(vector, metric, tiles, fitted, out):
    aux, height, width = tiles.shape[1:]
    column = jnp.sum(metric[...] * vector[0:1, :aux], axis=1, keepdims=True)
    fitted[...] = jnp.broadcast_to(column, (aux, width)).T[0:1, :]
    total = jnp.zeros((height, width), jnp.float32)
    for p in range(aux):
        total = total + column[p : p + 1, 0:1] * tiles[0, p].astype(jnp.float32)
    out[0] = total.astype(jnp.bfloat16)


def coulomb_tile(vector, metric_inv, three_index):
    aux, height, width = three_index.shape[1:]
    return pl.pallas_call(
        coulomb_kernel,
        out_shape=[
            jax.ShapeDtypeStruct((1, aux), jnp.float32),
            jax.ShapeDtypeStruct((1, height, width), jnp.bfloat16),
        ],
        compiler_params=pltpu.CompilerParams(vmem_limit_bytes=16 << 20),
        cost_estimate=SHORT,
    )(vector, metric_inv, three_index)


def finish_row(total, done, *backs):
    height = total.shape[0]
    done[...] = total.astype(jnp.bfloat16)
    for k, out in enumerate(backs):
        for b in range(2):
            at = (2 * k + b) * height
            out[b * height : (b + 1) * height, :] = total[:, at : at + height].T.astype(jnp.bfloat16)
        if out.shape[0] > 2 * height:
            out[2 * height :, :] = jnp.zeros((out.shape[0] - 2 * height, height), jnp.bfloat16)


def backs_of(group, height):
    return [
        jax.ShapeDtypeStruct((2 * height + spare_of(region), height), jnp.bfloat16)
        for region in returned(group)
    ]


def finish_early_kernel(own, vector, extra, code, done, *refs):
    height, columns = own.shape
    *backs, other_extra, vector_out = refs
    came = decode(code, 0, height)
    finish_row(own[...] + came[:, :columns], done, *backs)
    other_extra[...] = (extra[...] + came[:, columns:]).T.astype(jnp.bfloat16)
    vector_out[...] = vector[...] + decode_vector(code, vector.shape[1])


def finish_early(own, vector, extra, code):
    height = own.shape[0]
    shapes = [jax.ShapeDtypeStruct(own.shape, jnp.bfloat16)] + backs_of(Z_FIRST, height)
    shapes += [jax.ShapeDtypeStruct((height, height), jnp.bfloat16), sums_of(*vector.shape)]
    return small_call(finish_early_kernel, shapes, own, vector, extra, code)


def finish_late_kernel(own, code, done, *backs):
    finish_row(own[...] + decode(code, 0, own.shape[0]), done, *backs)


def finish_late(own, code, group, cost=SHORT):
    backs = backs_of(group, own.shape[0])
    return small_call(finish_late_kernel, [jax.ShapeDtypeStruct(own.shape, jnp.bfloat16)] + backs, own, code, cost=cost)


def give_back(blocks, region):
    came = lax.ppermute(blocks, "row", [(i, i ^ first_place(i, region)) for i in range(ROWS)])
    return came, send(came, CORE)


def return_all(backs, group):
    return sum((give_back(blocks, region) for blocks, region in zip(backs, returned(group))), ())


def assemble_kernel(holders, early, late, later, extra, extra_core, *refs):
    came, out = refs[:-1], refs[-1]
    width = early.shape[0]
    me = lax.axis_index("row")

    def put(place, block):
        where = pl.ds(pl.multiple_of(holders[place ^ me] * width, width), width)
        out[0, :, where] = block

    k = 0
    for group, rows in ((Z_FIRST, early), (SOONER, late), (LATER, later)):
        at = 0
        for region in group:
            start = first_place(me, region)
            for b in range(width_of(region)):
                put(start + b, rows[:, at * width : (at + 1) * width])
                at += 1
            if region in returned(group):
                start = region * 8 + 2 - start
                put(start, came[k][:width, :])
                put(start + 1, came[k + 1][width : 2 * width, :])
                k += 2
    put(5 - first_place(me, "extra"), jnp.where((me >> 1) & 1 == 0, extra_core[...], extra[...]))


def assemble(row_block, early, *rest):
    width = early.shape[0]
    vmem = pl.BlockSpec(memory_space=pltpu.VMEM)
    return pl.pallas_call(
        assemble_kernel,
        in_specs=[pl.BlockSpec(memory_space=pltpu.SMEM)] + [vmem] * (1 + len(rest)),
        out_shape=jax.ShapeDtypeStruct((1, width, ROWS * width), jnp.bfloat16),
        compiler_params=pltpu.CompilerParams(vmem_limit_bytes=16 << 20),
        cost_estimate=SHORT,
    )(row_block, early, *rest)


def naming(blocks, row_block, capacity):
    slots, orbits = blocks.shape
    holders = jnp.arange(ROWS, dtype=jnp.int32)
    hits = (blocks[:, :, None] == row_block[None, None, :]).astype(jnp.int32)
    rank = jnp.sum(hits * holders, axis=2)
    named = jnp.sum(hits, axis=0)
    code = jnp.arange(orbits, dtype=jnp.int32)[:, None] * 8 + jnp.sum(
        hits * jnp.arange(slots, dtype=jnp.int32)[:, None, None], axis=0
    )
    earlier = (jnp.arange(orbits)[None, :] < jnp.arange(orbits)[:, None]).astype(jnp.int32)
    before = jnp.sum(earlier[:, :, None] * named[None, :, :], axis=1)
    here = (before[:, :, None] == jnp.arange(capacity)) & (named[:, :, None] > 0)
    listed = jnp.sum(jnp.where(here, code[:, :, None] + 1, 0), axis=0) - 1
    return listed, rank


def summed_rows(panels, blocks, row_block, coeffs, metric_inv, three_index):
    orbits, slots, aux, width = panels.shape
    capacity = orbits * slots // ROWS

    other = send(panels, CORE)
    coeffs = coeffs.transpose(1, 0, 2)
    coeffs_other = send(coeffs, CORE)
    listed, rank = naming(blocks.T, row_block, capacity)
    listed_other, rank_other = send(listed, CORE), send(rank, CORE)
    listed, rank, panels = lax.optimization_barrier((listed, rank, panels))
    mine = bring(panels)
    ranks, sides = (rank, rank_other), (mine, other)

    jobs = ((SOONER, LATER), [Y] + [z | Y for z in Z], True), ((Z_FIRST,), [4 | Y, 4, 8 | Y, 8], True)
    late_go, later_go, early_go, vector = partial_rows(
        jobs, (listed, listed_other), ranks, sides, coeffs, coeffs_other
    )
    late_code = send(late_go, Y)
    early_code = send(early_go, NEAR)
    later_code = send(later_go, Y)

    listed, *_ = lax.optimization_barrier((listed, late_go, early_go, later_go))
    jobs = ((Z_FIRST,), [Y, 0, 12 | Y, 12], False), ((SOONER, LATER), [0, *Z], False)
    early_stay, late_stay, later_stay = partial_rows(jobs, (listed, listed_other), ranks, sides)

    early_stay, early_turn, vector = turn_near(early_stay, vector, early_code)
    early_code = send(early_turn, FAR)
    late, late_turn = turn_y(late_stay, late_code, 8)
    near_code = send(late_turn, NEAR)
    later, later_turn = turn_y(later_stay, later_code, 0)
    late, late_turn = turn_z(late, near_code, 8)
    late_code = send(late_turn, FAR)
    later, later_turn = turn_z(later, send(later_turn, NEAR), 0)
    later_code = send(later_turn, FAR)

    early_own, early_turn, vector, extra = turn_far(early_stay, vector, early_code)
    early, *early_back, extra, vector = finish_early(early_own, vector, extra, send(early_turn, Y))
    came = return_all(early_back, Z_FIRST)
    extra_core = send(extra, CORE)
    fitted, coulomb = coulomb_tile(vector, metric_inv, three_index)

    late, coulomb = lax.optimization_barrier((late, coulomb))
    late, *back = finish_late(late, late_code, SOONER)
    came += return_all(back, SOONER)
    later, *back = finish_late(later, later_code, LATER)
    came += return_all(back, LATER)
    exchange = assemble(row_block, early, late, later, extra, extra_core, *came)
    return (exchange, coulomb, fitted[0])


def solution(mesh):
    placed = (
        P(("groups", "row"), None, None, None),
        P(("groups", "row"), None),
        P("groups"),
        P(("groups", "row"), None, None),
        P("groups", None),
        P(("groups", "row"), None, None, None),
    )
    return jax.shard_map(
        summed_rows if mesh.shape["row"] == ROWS else sent_panels,
        mesh=mesh,
        in_specs=placed,
        out_specs=(P(("groups", "row"), None, None), P(("groups", "row"), None, None), P("groups")),
        check_vma=False,
    )
```

```python
import functools
import jax
import jax.numpy as jnp
from jax import lax
from jax.experimental import pallas as pl
from jax.experimental.pallas import tpu as pltpu
from jax.sharding import PartitionSpec as P


def row_terms(rows_in, row_ids, owned, count):
    total_rows = rows_in.shape[0]
    group = 32
    slots = rows_in.shape[1]
    width = rows_in.shape[3]
    grouped = rows_in.reshape((total_rows // group, group) + rows_in.shape[1:])
    grouped_ids = row_ids.reshape(total_rows // group, group, slots)

    def step(total, item):
        block_rows, block_ids = item
        chosen = (block_ids == owned).astype(jnp.bfloat16)
        picked = jnp.einsum(
            "gs,gspk->gpk", chosen, block_rows, preferred_element_type=jnp.float32
        ).astype(jnp.bfloat16)
        prods = jnp.einsum("gpk,gspn->gskn", picked, block_rows, preferred_element_type=jnp.float32)
        target = jnp.maximum(block_ids, 0).reshape(-1)
        added = jax.ops.segment_sum(prods.reshape(-1, width, width), target, num_segments=count)
        return (total + added, None)

    start = jnp.zeros((count, width, width), jnp.float32)
    total, _ = lax.scan(step, start, (grouped, grouped_ids))
    return total


def sent_panels(panels, blocks, row_block, coeffs, metric_inv, three_index):
    count = row_block.shape[0]
    orbits, slots, aux, width = panels.shape
    capacity = max(2, (orbits * slots + count - 1) // count)
    here = lax.axis_index("row")
    owned = row_block[here]
    ranks = jnp.arange(count, dtype=jnp.int32)
    flat_ids = blocks.reshape(-1)
    matches = (row_block[None, :] == flat_ids[:, None]).astype(jnp.int32)
    target = jnp.sum(matches * ranks[None, :], axis=1)
    hits = (ranks[None, :] == target[:, None]).astype(jnp.int32)
    before = jnp.cumsum(hits, axis=0) - hits
    place = jnp.sum(before * hits, axis=1)
    source = jnp.repeat(panels, slots, axis=0)
    source_ids = jnp.repeat(blocks, slots, axis=0).astype(jnp.bfloat16)
    outgoing = (
        jnp.zeros((count, capacity, slots, aux, width), jnp.bfloat16).at[target, place].set(source)
    )
    outgoing_ids = (
        jnp.full((count, capacity, slots), -1.0, jnp.bfloat16).at[target, place].set(source_ids)
    )
    partial_terms = jnp.einsum(
        "ispm,ism->p", panels.astype(jnp.float32), coeffs, precision=lax.Precision.HIGHEST
    )
    gamma = lax.psum(partial_terms, "row")
    fitted = jnp.dot(metric_inv, gamma, precision=lax.Precision.HIGHEST)
    coulomb = jnp.einsum(
        "p,rpmn->rmn", fitted, three_index.astype(jnp.float32), precision=lax.Precision.HIGHEST
    )
    arrived, arrived_ids = (
        lax.all_to_all(outgoing, "row", split_axis=0, concat_axis=0, tiled=True),
        lax.all_to_all(outgoing_ids, "row", split_axis=0, concat_axis=0, tiled=True),
    )
    accum = row_terms(
        arrived.reshape(-1, slots, aux, width),
        arrived_ids.reshape(-1, slots).astype(jnp.int32),
        owned,
        count,
    )
    exchange = accum.transpose(1, 0, 2).reshape(width, count * width)[None].astype(jnp.bfloat16)
    return (exchange, coulomb.astype(jnp.bfloat16), fitted)


ROWS = 16
CORE, Y, Z = 1, 2, (4, 8, 12)
NEAR = 4
EARLY_FAR, LATE_FAR, LATER_FAR = 8, 12, 12
PLACES = 16
Z_FIRST, SOONER, LATER = (3, "extra"), (1, "diagonal"), (2, "mate")
TAIL = 16
TOP = 14.99
SPARE = 0
VECTOR = 4
AHEAD = 6
SHORT = pl.CostEstimate(flops=1024, bytes_accessed=1024, transcendentals=0)
LONG = pl.CostEstimate(flops=1 << 32, bytes_accessed=1024, transcendentals=0)


def send(x, flip):
    return lax.ppermute(x, "row", [(i, i ^ flip) for i in range(ROWS)])


def side_of(z, apart):
    return (z >> 1) & 1 if apart == 2 else z & 1


def first_place(row, region):
    if region in ("diagonal", "mate"):
        return int(region == "mate")
    if region == "extra":
        return 2 + ((row >> 1) & 1)
    return region * 4 + side_of(row >> 2, region) * 2


def returned(group):
    return [region for region in group if region in (1, 2, 3)]


EXTRA_SPARE = 48


def spare_of(region):
    return {Z_FIRST[0]: 32, SOONER[0]: 16, LATER[0]: 0}[region]


def width_of(region):
    return 2 if region in (1, 2, 3) else 1


def encode(out, sums, vector=()):
    height, columns = sums[0].shape
    rest = out.shape[0] - len(sums) * height
    line = lax.broadcasted_iota(jnp.int32, (rest, columns), 0)
    tail = jnp.zeros((rest, columns), jnp.float32)
    for j, x in enumerate(sums):
        peak = jnp.maximum(jnp.max(jnp.abs(x), axis=0, keepdims=True), 2.0**-100)
        exponent = jnp.ceil(jnp.log2(peak) * 8)
        scaled = jnp.round(x * jnp.exp2(TOP - exponent * 0.125))
        out[j * height : (j + 1) * height, :] = scaled.astype(jnp.int32).astype(jnp.int16)
        tail = jnp.where(line == j, exponent, tail)
    for j, x in enumerate(vector):
        beside = jnp.zeros((1, columns - x.shape[1]), jnp.float32)
        tail = jnp.where(line == VECTOR + j, jnp.concatenate([x, beside], axis=1), tail)
    out[len(sums) * height :, :] = tail.astype(jnp.int32).astype(jnp.int16)


def encode_vector(x):
    exponent = jnp.ceil(jnp.log2(jnp.maximum(jnp.abs(x), 2.0**-100)))
    scaled = x * jnp.exp2(14 - exponent)
    high = jnp.round(scaled)
    low = jnp.round((scaled - high) * 2.0**15)
    return (exponent, high, low), combine(exponent, high, low)


def combine(exponent, high, low):
    return (high + low * 2.0**-15) * jnp.exp2(exponent - 14)


def decode_vector(codes, width):
    tail = codes[codes.shape[0] - TAIL :, :width].astype(jnp.int32).astype(jnp.float32)
    return combine(*(tail[VECTOR + j : VECTOR + j + 1, :] for j in range(3)))


def decode(codes, j, height):
    count = (codes.shape[0] - TAIL) // height
    exponents = codes[count * height :, :].astype(jnp.int32).astype(jnp.float32)
    scale = jnp.exp2(exponents[j : j + 1, :] * 0.125 - TOP)
    return codes[j * height : (j + 1) * height, :].astype(jnp.int32).astype(jnp.float32) * scale


def bring_kernel(far, near, arrived):
    copy = pltpu.make_async_copy(far, near, arrived)
    copy.start()
    copy.wait()


def bring(panels):
    return pl.pallas_call(
        bring_kernel,
        in_specs=[pl.BlockSpec(memory_space=pltpu.HBM)],
        out_specs=pl.BlockSpec(memory_space=pltpu.VMEM),
        out_shape=jax.ShapeDtypeStruct(panels.shape, panels.dtype),
        scratch_shapes=[pltpu.SemaphoreType.DMA],
        compiler_params=pltpu.CompilerParams(vmem_limit_bytes=16 << 20),
        cost_estimate=SHORT,
    )(panels)


def density_of(panels, coeffs):
    orbits, slots, aux, width = panels.shape
    total = jnp.zeros((aux, width), jnp.float32)
    for i in range(orbits):
        for t in range(slots):
            total = total + panels[i, t].astype(jnp.float32) * coeffs[t, i : i + 1, :]
    return total


def rows_kernel(jobs, project, listed, ranks, listed_other, ranks_other, mine, other_far, *refs):
    if project:
        coeffs, coeffs_other, refs = refs[0], refs[1], refs[2:]
    outs, (other, arrived), picks, spreads = refs[: -2 * AHEAD - 2], refs[-2:], refs[-2 * AHEAD - 2 : -AHEAD - 2], refs[-AHEAD - 2 : -2]
    orbits, slots, aux, width = mine.shape
    capacity = listed.shape[1]
    me = lax.axis_index("row")
    copy = pltpu.make_async_copy(other_far, other, arrived)
    copy.start()
    todo = [(job, j) for job in range(len(jobs)) for j in range(len(jobs[job][1]))]

    def spans_of(job, j):
        groups, flips, _ = jobs[job]
        return [
            [
                pl.ds(pl.multiple_of(first_place(me ^ flips[j], region) * width, width), width_of(region) * width)
                for region in group
            ]
            for group in groups
        ]

    def gather(step, side):
        job, j = todo[step]
        row = me ^ jobs[job][1][j]
        picked, spread = picks[step % AHEAD], spreads[step % AHEAD]
        names, places_of, panels = ((listed, ranks, mine), (listed_other, ranks_other, other))[side]
        half = capacity * aux
        for span in sum(spans_of(job, j), []):
            spread[side * half : (side + 1) * half, span] = jnp.zeros((half, span.size), jnp.bfloat16)
        for n in range(capacity):
            code = names[row, n]
            orbit, slot = jnp.maximum(code, 0) >> 3, jnp.maximum(code, 0) & 7
            at = pl.ds((side * capacity + n) * aux, aux)
            chosen = panels[orbit, slot]
            tiles = [panels[orbit, t] for t in range(slots)]
            places = [places_of[t, orbit] ^ row for t in range(slots)]
            picked[at, :] = jnp.where(code >= 0, chosen, jnp.zeros_like(chosen))
            for tile, place in zip(tiles, places):
                spread[at, pl.ds(pl.multiple_of(place * width, width), width)] = tile

    for step in range(min(AHEAD, len(todo))):
        gather(step, 0)
    if project:
        total = density_of(mine, coeffs)
    copy.wait()
    vector = ()
    if project:
        total = jnp.sum((total + density_of(other, coeffs_other)).T, axis=0, keepdims=True)
        total = jnp.concatenate([total, jnp.zeros((1, width - aux), jnp.float32)], axis=1)
        vector, outs[-1][...] = encode_vector(total)
    first, gathered = 0, {}
    for step, (job, j) in enumerate(todo):
        gather(step, 1)
        picked, spread = picks[step % AHEAD], spreads[step % AHEAD]
        sums = [
            [
                lax.dot_general(
                    picked[...],
                    spread[:, span],
                    (((0,), (0,)), ((), ())),
                    preferred_element_type=jnp.float32,
                )
                for span in spans
            ]
            for spans in spans_of(job, j)
        ]
        if step + AHEAD < len(todo):
            gather(step + AHEAD, 0)
        groups, flips, coded = jobs[job]
        for k, parts in enumerate(sums):
            out = outs[first + k]
            row = jnp.concatenate(parts, axis=1) if len(parts) > 1 else parts[0]
            if not coded:
                out[j] = row
                continue
            gathered.setdefault((job, k), []).append(row)
            if j + 1 == len(flips):
                encode(out, gathered[job, k], vector if job + 1 == len(jobs) else ())
        if j + 1 == len(flips):
            first += len(groups)


def partial_rows(jobs, lists, ranks, panels, *coeffs):
    orbits, slots, aux, width = panels[0].shape
    depth = 2 * lists[0].shape[1] * aux
    shapes = []
    for groups, flips, coded in jobs:
        for group in groups:
            columns = sum(width_of(region) for region in group) * width
            if coded:
                spare = SPARE if group == LATER else 0
                shapes.append(message_of(len(flips) * width, columns, spare))
            else:
                shapes.append(sums_of(len(flips), width, columns))
    if coeffs:
        shapes.append(jax.ShapeDtypeStruct((1, width), jnp.float32))
    scalars = pl.BlockSpec(memory_space=pltpu.SMEM)
    whole = pl.BlockSpec(memory_space=pltpu.VMEM)
    return pl.pallas_call(
        functools.partial(rows_kernel, jobs, len(coeffs)),
        in_specs=[scalars] * 4 + [whole, pl.BlockSpec(memory_space=pltpu.HBM)] + [whole] * len(coeffs),
        out_specs=[whole] * len(shapes),
        out_shape=shapes,
        scratch_shapes=[pltpu.VMEM((depth, width), jnp.bfloat16)] * AHEAD
        + [pltpu.VMEM((depth, PLACES * width), jnp.bfloat16)] * AHEAD
        + [pltpu.VMEM(panels[1].shape, jnp.bfloat16), pltpu.SemaphoreType.DMA],
        compiler_params=pltpu.CompilerParams(vmem_limit_bytes=28 << 20),
        cost_estimate=SHORT,
    )(lists[0], ranks[0], lists[1], ranks[1], *panels, *coeffs)


def turn_y_kernel(last, stay, code, kept, message):
    height = stay.shape[1]
    encode(message, [stay[j] + decode(code, j, height) for j in (1, 1 ^ last // 4)])
    for k, j in enumerate((0, last // 4)):
        kept[k] = stay[j] + decode(code, j, height)


def turn_z_kernel(kept, code, own, message):
    height = own.shape[0]
    encode(message, [kept[1] + decode(code, 1, height)])
    own[...] = kept[0] + decode(code, 0, height)


def turn_near_kernel(stay, projected, code, kept, message, vector):
    height = kept.shape[1]
    rows, vector[...] = encode_vector(projected[...] + decode_vector(code, projected.shape[1]))
    encode(message, [stay[j] + decode(code, j, height) for j in (2, 3)], rows)
    for j in range(2):
        kept[j] = stay[j] + decode(code, j, height)


def turn_far_kernel(stay, projected, code, own, message, vector, extra):
    height, width = own.shape[0], extra.shape[1]
    rows, vector[...] = encode_vector(projected[...] + decode_vector(code, projected.shape[1]))
    theirs, mine = [stay[j] + decode(code, j, height) for j in range(2)]
    encode(message, [jnp.concatenate([theirs, mine[:, -width:]], axis=1)], rows)
    own[...] = mine
    extra[...] = theirs[:, -width:]


def message_of(rows, columns, spare=0):
    return jax.ShapeDtypeStruct((rows + TAIL + spare, columns), jnp.int16)


def small_call(kernel, shapes, *args, cost=SHORT):
    return pl.pallas_call(
        kernel,
        out_shape=shapes,
        compiler_params=pltpu.CompilerParams(vmem_limit_bytes=16 << 20),
        cost_estimate=cost,
    )(*args)


def sums_of(*shape):
    return jax.ShapeDtypeStruct(shape, jnp.float32)


def turn_y(stay, code, spare, last):
    height, columns = stay.shape[1:]
    shapes = [sums_of(2, height, columns), message_of(2 * height, columns, spare)]
    return small_call(functools.partial(turn_y_kernel, last), shapes, stay, code)


def turn_z(kept, code, spare):
    height, columns = kept.shape[1:]
    shapes = [sums_of(height, columns), message_of(height, columns, spare)]
    return small_call(turn_z_kernel, shapes, kept, code)


def turn_near(stay, projected, code):
    height, columns = stay.shape[1:]
    shapes = [sums_of(2, height, columns), message_of(2 * height, columns), sums_of(1, projected.shape[1])]
    return small_call(turn_near_kernel, shapes, stay, projected, code)


def turn_far(stay, projected, code):
    height, columns = stay.shape[1:]
    shapes = [sums_of(height, columns), message_of(height, columns + height), sums_of(*projected.shape)]
    shapes.append(sums_of(height, height))
    return small_call(turn_far_kernel, shapes, stay, projected, code)


def coulomb_kernel(vector, metric, tiles, fitted, out):
    aux, height, width = tiles.shape[1:]
    column = jnp.sum(metric[...] * vector[0:1, :aux], axis=1, keepdims=True)
    fitted[...] = jnp.broadcast_to(column, (aux, width)).T[0:1, :]
    total = jnp.zeros((height, width), jnp.float32)
    for p in range(aux):
        total = total + column[p : p + 1, 0:1] * tiles[0, p].astype(jnp.float32)
    out[0] = total.astype(jnp.bfloat16)


def coulomb_tile(vector, metric_inv, three_index):
    aux, height, width = three_index.shape[1:]
    return pl.pallas_call(
        coulomb_kernel,
        out_shape=[
            jax.ShapeDtypeStruct((1, aux), jnp.float32),
            jax.ShapeDtypeStruct((1, height, width), jnp.bfloat16),
        ],
        compiler_params=pltpu.CompilerParams(vmem_limit_bytes=16 << 20),
        cost_estimate=SHORT,
    )(vector, metric_inv, three_index)


def finish_row(total, done, *backs):
    height = total.shape[0]
    done[...] = total.astype(jnp.bfloat16)
    for k, out in enumerate(backs):
        for b in range(2):
            at = (2 * k + b) * height
            out[b * height : (b + 1) * height, :] = total[:, at : at + height].T.astype(jnp.bfloat16)
        if out.shape[0] > 2 * height:
            out[2 * height :, :] = jnp.zeros((out.shape[0] - 2 * height, height), jnp.bfloat16)


def backs_of(group, height):
    return [
        jax.ShapeDtypeStruct((2 * height + spare_of(region), height), jnp.bfloat16)
        for region in returned(group)
    ]


def finish_early_kernel(own, vector, extra, code, done, *refs):
    height, columns = own.shape
    *backs, other_extra, vector_out = refs
    came = decode(code, 0, height)
    finish_row(own[...] + came[:, :columns], done, *backs)
    other_extra[:height, :] = (extra[...] + came[:, columns:]).T.astype(jnp.bfloat16)
    other_extra[height:, :] = jnp.zeros((other_extra.shape[0] - height, height), jnp.bfloat16)
    vector_out[...] = vector[...] + decode_vector(code, vector.shape[1])


def finish_early(own, vector, extra, code):
    height = own.shape[0]
    shapes = [jax.ShapeDtypeStruct(own.shape, jnp.bfloat16)] + backs_of(Z_FIRST, height)
    shapes += [jax.ShapeDtypeStruct((2 * height + EXTRA_SPARE, height), jnp.bfloat16), sums_of(*vector.shape)]
    return small_call(finish_early_kernel, shapes, own, vector, extra, code)


def finish_late_kernel(own, code, done, *backs):
    finish_row(own[...] + decode(code, 0, own.shape[0]), done, *backs)


def finish_late(own, code, group, cost=SHORT):
    backs = backs_of(group, own.shape[0])
    return small_call(finish_late_kernel, [jax.ShapeDtypeStruct(own.shape, jnp.bfloat16)] + backs, own, code, cost=cost)


def give_back(blocks, region):
    came = lax.ppermute(blocks, "row", [(i, i ^ first_place(i, region)) for i in range(ROWS)])
    return came, send(came, CORE)


def return_all(backs, group):
    return sum((give_back(blocks, region) for blocks, region in zip(backs, returned(group))), ())


def assemble_kernel(holders, early, late, later, extra, extra_core, *refs):
    came, out = refs[:-1], refs[-1]
    width = early.shape[0]
    me = lax.axis_index("row")

    def put(place, block):
        where = pl.ds(pl.multiple_of(holders[place ^ me] * width, width), width)
        out[0, :, where] = block

    k = 0
    for group, rows in ((Z_FIRST, early), (SOONER, late), (LATER, later)):
        at = 0
        for region in group:
            start = first_place(me, region)
            for b in range(width_of(region)):
                put(start + b, rows[:, at * width : (at + 1) * width])
                at += 1
            if region in returned(group):
                start = region * 8 + 2 - start
                put(start, came[k][:width, :])
                put(start + 1, came[k + 1][width : 2 * width, :])
                k += 2
    put(5 - first_place(me, "extra"), jnp.where((me >> 1) & 1 == 0, extra_core[:width, :], extra[:width, :]))


def assemble(row_block, early, *rest):
    width = early.shape[0]
    vmem = pl.BlockSpec(memory_space=pltpu.VMEM)
    return pl.pallas_call(
        assemble_kernel,
        in_specs=[pl.BlockSpec(memory_space=pltpu.SMEM)] + [vmem] * (1 + len(rest)),
        out_shape=jax.ShapeDtypeStruct((1, width, ROWS * width), jnp.bfloat16),
        compiler_params=pltpu.CompilerParams(vmem_limit_bytes=16 << 20),
        cost_estimate=SHORT,
    )(row_block, early, *rest)


def naming(blocks, row_block, capacity):
    slots, orbits = blocks.shape
    holders = jnp.arange(ROWS, dtype=jnp.int32)
    hits = (blocks[:, :, None] == row_block[None, None, :]).astype(jnp.int32)
    rank = jnp.sum(hits * holders, axis=2)
    named = jnp.sum(hits, axis=0)
    code = jnp.arange(orbits, dtype=jnp.int32)[:, None] * 8 + jnp.sum(
        hits * jnp.arange(slots, dtype=jnp.int32)[:, None, None], axis=0
    )
    earlier = (jnp.arange(orbits)[None, :] < jnp.arange(orbits)[:, None]).astype(jnp.int32)
    before = jnp.sum(earlier[:, :, None] * named[None, :, :], axis=1)
    here = (before[:, :, None] == jnp.arange(capacity)) & (named[:, :, None] > 0)
    listed = jnp.sum(jnp.where(here, code[:, :, None] + 1, 0), axis=0) - 1
    return listed, rank


def summed_rows(panels, blocks, row_block, coeffs, metric_inv, three_index):
    orbits, slots, aux, width = panels.shape
    capacity = orbits * slots // ROWS

    other = send(panels, CORE)
    coeffs = coeffs.transpose(1, 0, 2)
    coeffs_other = send(coeffs, CORE)
    listed, rank = naming(blocks.T, row_block, capacity)
    listed_other, rank_other = send(listed, CORE), send(rank, CORE)
    listed, rank, panels = lax.optimization_barrier((listed, rank, panels))
    mine = bring(panels)
    ranks, sides = (rank, rank_other), (mine, other)

    jobs = ((SOONER, LATER), [Y] + [z | Y for z in Z], True), ((Z_FIRST,), [4 | Y, 4, (4 ^ EARLY_FAR) | Y, 4 ^ EARLY_FAR], True)
    late_go, later_go, early_go, vector = partial_rows(
        jobs, (listed, listed_other), ranks, sides, coeffs, coeffs_other
    )
    late_code = send(late_go, Y)
    early_code = send(early_go, NEAR)
    later_code = send(later_go, Y)

    listed, *_ = lax.optimization_barrier((listed, late_go, early_go, later_go))
    jobs = ((Z_FIRST,), [Y, 0, EARLY_FAR | Y, EARLY_FAR], False), ((SOONER, LATER), [0, *Z], False)
    early_stay, late_stay, later_stay = partial_rows(jobs, (listed, listed_other), ranks, sides)

    early_stay, early_turn, vector = turn_near(early_stay, vector, early_code)
    early_code = send(early_turn, EARLY_FAR)
    late, late_turn = turn_y(late_stay, late_code, 16, LATE_FAR)
    near_code = send(late_turn, NEAR)
    later, later_turn = turn_y(later_stay, later_code, 0, LATER_FAR)
    late, late_turn = turn_z(late, near_code, 0)
    late_code = send(late_turn, LATE_FAR)
    later, later_turn = turn_z(later, send(later_turn, NEAR), 0)
    later_code = send(later_turn, LATER_FAR)

    early_own, early_turn, vector, extra = turn_far(early_stay, vector, early_code)
    early, *early_back, extra, vector = finish_early(early_own, vector, extra, send(early_turn, Y))
    came = return_all(early_back, Z_FIRST)
    extra_core = send(extra, CORE)
    fitted, coulomb = coulomb_tile(vector, metric_inv, three_index)

    late, coulomb = lax.optimization_barrier((late, coulomb))
    late, *back = finish_late(late, late_code, SOONER)
    came += return_all(back, SOONER)
    later, *back = finish_late(later, later_code, LATER)
    came += return_all(back, LATER)
    exchange = assemble(row_block, early, late, later, extra, extra_core, *came)
    return (exchange, coulomb, fitted[0])


def solution(mesh):
    placed = (
        P(("groups", "row"), None, None, None),
        P(("groups", "row"), None),
        P("groups"),
        P(("groups", "row"), None, None),
        P("groups", None),
        P(("groups", "row"), None, None, None),
    )
    return jax.shard_map(
        summed_rows if mesh.shape["row"] == ROWS else sent_panels,
        mesh=mesh,
        in_specs=placed,
        out_specs=(P(("groups", "row"), None, None), P(("groups", "row"), None, None), P("groups")),
        check_vma=False,
    )
```

```python
import functools
import jax
import jax.numpy as jnp
from jax import lax
from jax.experimental import pallas as pl
from jax.experimental.pallas import tpu as pltpu
from jax.sharding import PartitionSpec as P


def row_terms(rows_in, row_ids, owned, count):
    total_rows = rows_in.shape[0]
    group = 32
    slots = rows_in.shape[1]
    width = rows_in.shape[3]
    grouped = rows_in.reshape((total_rows // group, group) + rows_in.shape[1:])
    grouped_ids = row_ids.reshape(total_rows // group, group, slots)

    def step(total, item):
        block_rows, block_ids = item
        chosen = (block_ids == owned).astype(jnp.bfloat16)
        picked = jnp.einsum(
            "gs,gspk->gpk", chosen, block_rows, preferred_element_type=jnp.float32
        ).astype(jnp.bfloat16)
        prods = jnp.einsum("gpk,gspn->gskn", picked, block_rows, preferred_element_type=jnp.float32)
        target = jnp.maximum(block_ids, 0).reshape(-1)
        added = jax.ops.segment_sum(prods.reshape(-1, width, width), target, num_segments=count)
        return (total + added, None)

    start = jnp.zeros((count, width, width), jnp.float32)
    total, _ = lax.scan(step, start, (grouped, grouped_ids))
    return total


def sent_panels(panels, blocks, row_block, coeffs, metric_inv, three_index):
    count = row_block.shape[0]
    orbits, slots, aux, width = panels.shape
    capacity = max(2, (orbits * slots + count - 1) // count)
    here = lax.axis_index("row")
    owned = row_block[here]
    ranks = jnp.arange(count, dtype=jnp.int32)
    flat_ids = blocks.reshape(-1)
    matches = (row_block[None, :] == flat_ids[:, None]).astype(jnp.int32)
    target = jnp.sum(matches * ranks[None, :], axis=1)
    hits = (ranks[None, :] == target[:, None]).astype(jnp.int32)
    before = jnp.cumsum(hits, axis=0) - hits
    place = jnp.sum(before * hits, axis=1)
    source = jnp.repeat(panels, slots, axis=0)
    source_ids = jnp.repeat(blocks, slots, axis=0).astype(jnp.bfloat16)
    outgoing = (
        jnp.zeros((count, capacity, slots, aux, width), jnp.bfloat16).at[target, place].set(source)
    )
    outgoing_ids = (
        jnp.full((count, capacity, slots), -1.0, jnp.bfloat16).at[target, place].set(source_ids)
    )
    partial_terms = jnp.einsum(
        "ispm,ism->p", panels.astype(jnp.float32), coeffs, precision=lax.Precision.HIGHEST
    )
    gamma = lax.psum(partial_terms, "row")
    fitted = jnp.dot(metric_inv, gamma, precision=lax.Precision.HIGHEST)
    coulomb = jnp.einsum(
        "p,rpmn->rmn", fitted, three_index.astype(jnp.float32), precision=lax.Precision.HIGHEST
    )
    arrived, arrived_ids = (
        lax.all_to_all(outgoing, "row", split_axis=0, concat_axis=0, tiled=True),
        lax.all_to_all(outgoing_ids, "row", split_axis=0, concat_axis=0, tiled=True),
    )
    accum = row_terms(
        arrived.reshape(-1, slots, aux, width),
        arrived_ids.reshape(-1, slots).astype(jnp.int32),
        owned,
        count,
    )
    exchange = accum.transpose(1, 0, 2).reshape(width, count * width)[None].astype(jnp.bfloat16)
    return (exchange, coulomb.astype(jnp.bfloat16), fitted)


ROWS = 16
CORE, Y, Z = 1, 2, (4, 8, 12)
NEAR = 4
EARLY_FAR, LATE_FAR, LATER_FAR = 8, 12, 12
PLACES = 16
Z_FIRST, SOONER, LATER = (3, "extra"), (1, "diagonal"), (2, "mate")
TAIL = 16
TOP = 14.99
SPARE = 0
VECTOR = 4
AHEAD = 6
SHORT = pl.CostEstimate(flops=1024, bytes_accessed=1024, transcendentals=0)
LONG = pl.CostEstimate(flops=1 << 32, bytes_accessed=1024, transcendentals=0)


def send(x, flip):
    return lax.ppermute(x, "row", [(i, i ^ flip) for i in range(ROWS)])


def side_of(z, apart):
    return (z >> 1) & 1 if apart == 2 else z & 1


def first_place(row, region):
    if region in ("diagonal", "mate"):
        return int(region == "mate")
    if region == "extra":
        return 2 + ((row >> 1) & 1)
    return region * 4 + side_of(row >> 2, region) * 2


def returned(group):
    return [region for region in group if region in (1, 2, 3)]


EXTRA_SPARE = 48


def spare_of(region):
    return {Z_FIRST[0]: 32, SOONER[0]: 16, LATER[0]: 0}[region]


def width_of(region):
    return 2 if region in (1, 2, 3) else 1


def encode_row(out, j, x, tail):
    height, columns = x.shape
    if tail is None:
        tail = jnp.zeros((out.shape[0] % height, columns), jnp.float32)
    peak = jnp.maximum(jnp.max(jnp.abs(x), axis=0, keepdims=True), 2.0**-100)
    exponent = jnp.ceil(jnp.log2(peak) * 8)
    scaled = jnp.round(x * jnp.exp2(TOP - exponent * 0.125))
    out[j * height : (j + 1) * height, :] = scaled.astype(jnp.int32).astype(jnp.int16)
    return jnp.where(lax.broadcasted_iota(jnp.int32, tail.shape, 0) == j, exponent, tail)


def encode_tail(out, tail, vector=()):
    rest, columns = tail.shape
    line = lax.broadcasted_iota(jnp.int32, tail.shape, 0)
    for j, x in enumerate(vector):
        beside = jnp.zeros((1, columns - x.shape[1]), jnp.float32)
        tail = jnp.where(line == VECTOR + j, jnp.concatenate([x, beside], axis=1), tail)
    out[out.shape[0] - rest :, :] = tail.astype(jnp.int32).astype(jnp.int16)


def encode(out, sums, vector=()):
    tail = None
    for j, x in enumerate(sums):
        tail = encode_row(out, j, x, tail)
    encode_tail(out, tail, vector)


def encode_vector(x):
    exponent = jnp.ceil(jnp.log2(jnp.maximum(jnp.abs(x), 2.0**-100)))
    scaled = x * jnp.exp2(14 - exponent)
    high = jnp.round(scaled)
    low = jnp.round((scaled - high) * 2.0**15)
    return (exponent, high, low), combine(exponent, high, low)


def combine(exponent, high, low):
    return (high + low * 2.0**-15) * jnp.exp2(exponent - 14)


def decode_vector(codes, width):
    tail = codes[codes.shape[0] - TAIL :, :width].astype(jnp.int32).astype(jnp.float32)
    return combine(*(tail[VECTOR + j : VECTOR + j + 1, :] for j in range(3)))


def decode(codes, j, height):
    count = (codes.shape[0] - TAIL) // height
    exponents = codes[count * height :, :].astype(jnp.int32).astype(jnp.float32)
    scale = jnp.exp2(exponents[j : j + 1, :] * 0.125 - TOP)
    return codes[j * height : (j + 1) * height, :].astype(jnp.int32).astype(jnp.float32) * scale


def bring_kernel(far, near, arrived):
    copy = pltpu.make_async_copy(far, near, arrived)
    copy.start()
    copy.wait()


def bring(panels):
    return pl.pallas_call(
        bring_kernel,
        in_specs=[pl.BlockSpec(memory_space=pltpu.HBM)],
        out_specs=pl.BlockSpec(memory_space=pltpu.VMEM),
        out_shape=jax.ShapeDtypeStruct(panels.shape, panels.dtype),
        scratch_shapes=[pltpu.SemaphoreType.DMA],
        compiler_params=pltpu.CompilerParams(vmem_limit_bytes=16 << 20),
        cost_estimate=SHORT,
    )(panels)


def density_of(panels, coeffs):
    orbits, slots, aux, width = panels.shape
    total = jnp.zeros((aux, width), jnp.float32)
    for i in range(orbits):
        for t in range(slots):
            total = total + panels[i, t].astype(jnp.float32) * coeffs[t, i : i + 1, :]
    return total


def rows_kernel(jobs, project, listed, ranks, listed_other, ranks_other, mine, other_far, *refs):
    if project:
        coeffs, coeffs_other, refs = refs[0], refs[1], refs[2:]
    outs, (other, arrived), picks, spreads = refs[: -2 * AHEAD - 2], refs[-2:], refs[-2 * AHEAD - 2 : -AHEAD - 2], refs[-AHEAD - 2 : -2]
    orbits, slots, aux, width = mine.shape
    capacity = listed.shape[1]
    me = lax.axis_index("row")
    copy = pltpu.make_async_copy(other_far, other, arrived)
    copy.start()
    todo = [(job, j) for job in range(len(jobs)) for j in range(len(jobs[job][1]))]

    def spans_of(job, j):
        groups, flips, _ = jobs[job]
        return [
            [
                pl.ds(pl.multiple_of(first_place(me ^ flips[j], region) * width, width), width_of(region) * width)
                for region in group
            ]
            for group in groups
        ]

    def gather(step, side):
        job, j = todo[step]
        row = me ^ jobs[job][1][j]
        picked, spread = picks[step % AHEAD], spreads[step % AHEAD]
        names, places_of, panels = ((listed, ranks, mine), (listed_other, ranks_other, other))[side]
        half = capacity * aux
        for span in sum(spans_of(job, j), []):
            spread[side * half : (side + 1) * half, span] = jnp.zeros((half, span.size), jnp.bfloat16)
        for n in range(capacity):
            code = names[row, n]
            orbit, slot = jnp.maximum(code, 0) >> 3, jnp.maximum(code, 0) & 7
            at = pl.ds((side * capacity + n) * aux, aux)
            chosen = panels[orbit, slot]
            tiles = [panels[orbit, t] for t in range(slots)]
            places = [places_of[t, orbit] ^ row for t in range(slots)]
            picked[at, :] = jnp.where(code >= 0, chosen, jnp.zeros_like(chosen))
            for tile, place in zip(tiles, places):
                spread[at, pl.ds(pl.multiple_of(place * width, width), width)] = tile

    for step in range(min(AHEAD, len(todo))):
        gather(step, 0)
    if project:
        total = density_of(mine, coeffs)
    copy.wait()
    vector = ()
    if project:
        total = jnp.sum((total + density_of(other, coeffs_other)).T, axis=0, keepdims=True)
        total = jnp.concatenate([total, jnp.zeros((1, width - aux), jnp.float32)], axis=1)
        vector, outs[-1][...] = encode_vector(total)
    first, tails = 0, {}
    for step, (job, j) in enumerate(todo):
        gather(step, 1)
        picked, spread = picks[step % AHEAD], spreads[step % AHEAD]
        sums = [
            [
                lax.dot_general(
                    picked[...],
                    spread[:, span],
                    (((0,), (0,)), ((), ())),
                    preferred_element_type=jnp.float32,
                )
                for span in spans
            ]
            for spans in spans_of(job, j)
        ]
        if step + AHEAD < len(todo):
            gather(step + AHEAD, 0)
        groups, flips, coded = jobs[job]
        for k, parts in enumerate(sums):
            out = outs[first + k]
            row = jnp.concatenate(parts, axis=1) if len(parts) > 1 else parts[0]
            if not coded:
                out[j] = row
                continue
            tails[job, k] = encode_row(out, j, row, tails.get((job, k)))
            if j + 1 == len(flips):
                encode_tail(out, tails[job, k], vector if job + 1 == len(jobs) else ())
        if j + 1 == len(flips):
            first += len(groups)


def partial_rows(jobs, lists, ranks, panels, *coeffs):
    orbits, slots, aux, width = panels[0].shape
    depth = 2 * lists[0].shape[1] * aux
    shapes = []
    for groups, flips, coded in jobs:
        for group in groups:
            columns = sum(width_of(region) for region in group) * width
            if coded:
                spare = SPARE if group == LATER else 0
                shapes.append(message_of(len(flips) * width, columns, spare))
            else:
                shapes.append(sums_of(len(flips), width, columns))
    if coeffs:
        shapes.append(jax.ShapeDtypeStruct((1, width), jnp.float32))
    scalars = pl.BlockSpec(memory_space=pltpu.SMEM)
    whole = pl.BlockSpec(memory_space=pltpu.VMEM)
    return pl.pallas_call(
        functools.partial(rows_kernel, jobs, len(coeffs)),
        in_specs=[scalars] * 4 + [whole, pl.BlockSpec(memory_space=pltpu.HBM)] + [whole] * len(coeffs),
        out_specs=[whole] * len(shapes),
        out_shape=shapes,
        scratch_shapes=[pltpu.VMEM((depth, width), jnp.bfloat16)] * AHEAD
        + [pltpu.VMEM((depth, PLACES * width), jnp.bfloat16)] * AHEAD
        + [pltpu.VMEM(panels[1].shape, jnp.bfloat16), pltpu.SemaphoreType.DMA],
        compiler_params=pltpu.CompilerParams(vmem_limit_bytes=28 << 20),
        cost_estimate=SHORT,
    )(lists[0], ranks[0], lists[1], ranks[1], *panels, *coeffs)


def turn_y_kernel(last, stay, code, kept, message):
    height = stay.shape[1]
    encode(message, [stay[j] + decode(code, j, height) for j in (1, 1 ^ last // 4)])
    for k, j in enumerate((0, last // 4)):
        kept[k] = stay[j] + decode(code, j, height)


def turn_z_kernel(kept, code, own, message):
    height = own.shape[0]
    encode(message, [kept[1] + decode(code, 1, height)])
    own[...] = kept[0] + decode(code, 0, height)


def turn_near_kernel(stay, projected, code, kept, message, vector):
    height = kept.shape[1]
    rows, vector[...] = encode_vector(projected[...] + decode_vector(code, projected.shape[1]))
    encode(message, [stay[j] + decode(code, j, height) for j in (2, 3)], rows)
    for j in range(2):
        kept[j] = stay[j] + decode(code, j, height)


def turn_far_kernel(stay, projected, code, own, message, vector, extra):
    height, width = own.shape[0], extra.shape[1]
    rows, vector[...] = encode_vector(projected[...] + decode_vector(code, projected.shape[1]))
    theirs, mine = [stay[j] + decode(code, j, height) for j in range(2)]
    encode(message, [jnp.concatenate([theirs, mine[:, -width:]], axis=1)], rows)
    own[...] = mine
    extra[...] = theirs[:, -width:]


def message_of(rows, columns, spare=0):
    return jax.ShapeDtypeStruct((rows + TAIL + spare, columns), jnp.int16)


def small_call(kernel, shapes, *args, cost=SHORT):
    return pl.pallas_call(
        kernel,
        out_shape=shapes,
        compiler_params=pltpu.CompilerParams(vmem_limit_bytes=16 << 20),
        cost_estimate=cost,
    )(*args)


def sums_of(*shape):
    return jax.ShapeDtypeStruct(shape, jnp.float32)


def turn_y(stay, code, spare, last):
    height, columns = stay.shape[1:]
    shapes = [sums_of(2, height, columns), message_of(2 * height, columns, spare)]
    return small_call(functools.partial(turn_y_kernel, last), shapes, stay, code)


def turn_z(kept, code, spare):
    height, columns = kept.shape[1:]
    shapes = [sums_of(height, columns), message_of(height, columns, spare)]
    return small_call(turn_z_kernel, shapes, kept, code)


def turn_near(stay, projected, code):
    height, columns = stay.shape[1:]
    shapes = [sums_of(2, height, columns), message_of(2 * height, columns), sums_of(1, projected.shape[1])]
    return small_call(turn_near_kernel, shapes, stay, projected, code)


def turn_far(stay, projected, code):
    height, columns = stay.shape[1:]
    shapes = [sums_of(height, columns), message_of(height, columns + height), sums_of(*projected.shape)]
    shapes.append(sums_of(height, height))
    return small_call(turn_far_kernel, shapes, stay, projected, code)


def coulomb_kernel(vector, metric, tiles, fitted, out):
    aux, height, width = tiles.shape[1:]
    column = jnp.sum(metric[...] * vector[0:1, :aux], axis=1, keepdims=True)
    fitted[...] = jnp.broadcast_to(column, (aux, width)).T[0:1, :]
    total = jnp.zeros((height, width), jnp.float32)
    for p in range(aux):
        total = total + column[p : p + 1, 0:1] * tiles[0, p].astype(jnp.float32)
    out[0] = total.astype(jnp.bfloat16)


def coulomb_tile(vector, metric_inv, three_index):
    aux, height, width = three_index.shape[1:]
    return pl.pallas_call(
        coulomb_kernel,
        out_shape=[
            jax.ShapeDtypeStruct((1, aux), jnp.float32),
            jax.ShapeDtypeStruct((1, height, width), jnp.bfloat16),
        ],
        compiler_params=pltpu.CompilerParams(vmem_limit_bytes=16 << 20),
        cost_estimate=SHORT,
    )(vector, metric_inv, three_index)


def finish_row(total, done, *backs):
    height = total.shape[0]
    done[...] = total.astype(jnp.bfloat16)
    for k, out in enumerate(backs):
        for b in range(2):
            at = (2 * k + b) * height
            out[b * height : (b + 1) * height, :] = total[:, at : at + height].T.astype(jnp.bfloat16)
        if out.shape[0] > 2 * height:
            out[2 * height :, :] = jnp.zeros((out.shape[0] - 2 * height, height), jnp.bfloat16)


def backs_of(group, height):
    return [
        jax.ShapeDtypeStruct((2 * height + spare_of(region), height), jnp.bfloat16)
        for region in returned(group)
    ]


def finish_early_kernel(own, vector, extra, code, done, *refs):
    height, columns = own.shape
    *backs, other_extra, vector_out = refs
    came = decode(code, 0, height)
    finish_row(own[...] + came[:, :columns], done, *backs)
    other_extra[:height, :] = (extra[...] + came[:, columns:]).T.astype(jnp.bfloat16)
    other_extra[height:, :] = jnp.zeros((other_extra.shape[0] - height, height), jnp.bfloat16)
    vector_out[...] = vector[...] + decode_vector(code, vector.shape[1])


def finish_early(own, vector, extra, code):
    height = own.shape[0]
    shapes = [jax.ShapeDtypeStruct(own.shape, jnp.bfloat16)] + backs_of(Z_FIRST, height)
    shapes += [jax.ShapeDtypeStruct((2 * height + EXTRA_SPARE, height), jnp.bfloat16), sums_of(*vector.shape)]
    return small_call(finish_early_kernel, shapes, own, vector, extra, code)


def finish_late_kernel(own, code, done, *backs):
    finish_row(own[...] + decode(code, 0, own.shape[0]), done, *backs)


def finish_late(own, code, group, cost=SHORT):
    backs = backs_of(group, own.shape[0])
    return small_call(finish_late_kernel, [jax.ShapeDtypeStruct(own.shape, jnp.bfloat16)] + backs, own, code, cost=cost)


def give_back(blocks, region):
    came = lax.ppermute(blocks, "row", [(i, i ^ first_place(i, region)) for i in range(ROWS)])
    return came, send(came, CORE)


def return_all(backs, group):
    return sum((give_back(blocks, region) for blocks, region in zip(backs, returned(group))), ())


def assemble_kernel(holders, early, late, later, extra, extra_core, *refs):
    came, out = refs[:-1], refs[-1]
    width = early.shape[0]
    me = lax.axis_index("row")

    def put(place, block):
        where = pl.ds(pl.multiple_of(holders[place ^ me] * width, width), width)
        out[0, :, where] = block

    k = 0
    for group, rows in ((Z_FIRST, early), (SOONER, late), (LATER, later)):
        at = 0
        for region in group:
            start = first_place(me, region)
            for b in range(width_of(region)):
                put(start + b, rows[:, at * width : (at + 1) * width])
                at += 1
            if region in returned(group):
                start = region * 8 + 2 - start
                put(start, came[k][:width, :])
                put(start + 1, came[k + 1][width : 2 * width, :])
                k += 2
    put(5 - first_place(me, "extra"), jnp.where((me >> 1) & 1 == 0, extra_core[:width, :], extra[:width, :]))


def assemble(row_block, early, *rest):
    width = early.shape[0]
    vmem = pl.BlockSpec(memory_space=pltpu.VMEM)
    return pl.pallas_call(
        assemble_kernel,
        in_specs=[pl.BlockSpec(memory_space=pltpu.SMEM)] + [vmem] * (1 + len(rest)),
        out_shape=jax.ShapeDtypeStruct((1, width, ROWS * width), jnp.bfloat16),
        compiler_params=pltpu.CompilerParams(vmem_limit_bytes=16 << 20),
        cost_estimate=SHORT,
    )(row_block, early, *rest)


def naming(blocks, row_block, capacity):
    slots, orbits = blocks.shape
    holders = jnp.arange(ROWS, dtype=jnp.int32)
    hits = (blocks[:, :, None] == row_block[None, None, :]).astype(jnp.int32)
    rank = jnp.sum(hits * holders, axis=2)
    named = jnp.sum(hits, axis=0)
    code = jnp.arange(orbits, dtype=jnp.int32)[:, None] * 8 + jnp.sum(
        hits * jnp.arange(slots, dtype=jnp.int32)[:, None, None], axis=0
    )
    earlier = (jnp.arange(orbits)[None, :] < jnp.arange(orbits)[:, None]).astype(jnp.int32)
    before = jnp.sum(earlier[:, :, None] * named[None, :, :], axis=1)
    here = (before[:, :, None] == jnp.arange(capacity)) & (named[:, :, None] > 0)
    listed = jnp.sum(jnp.where(here, code[:, :, None] + 1, 0), axis=0) - 1
    return listed, rank


def summed_rows(panels, blocks, row_block, coeffs, metric_inv, three_index):
    orbits, slots, aux, width = panels.shape
    capacity = orbits * slots // ROWS

    other = send(panels, CORE)
    coeffs = coeffs.transpose(1, 0, 2)
    coeffs_other = send(coeffs, CORE)
    listed, rank = naming(blocks.T, row_block, capacity)
    listed_other, rank_other = send(listed, CORE), send(rank, CORE)
    listed, rank, panels = lax.optimization_barrier((listed, rank, panels))
    mine = bring(panels)
    ranks, sides = (rank, rank_other), (mine, other)

    jobs = ((SOONER, LATER), [Y] + [z | Y for z in Z], True), ((Z_FIRST,), [4 | Y, 4, (4 ^ EARLY_FAR) | Y, 4 ^ EARLY_FAR], True)
    late_go, later_go, early_go, vector = partial_rows(
        jobs, (listed, listed_other), ranks, sides, coeffs, coeffs_other
    )
    late_code = send(late_go, Y)
    early_code = send(early_go, NEAR)
    later_code = send(later_go, Y)

    listed, *_ = lax.optimization_barrier((listed, late_go, early_go, later_go))
    jobs = ((Z_FIRST,), [Y, 0, EARLY_FAR | Y, EARLY_FAR], False), ((SOONER, LATER), [0, *Z], False)
    early_stay, late_stay, later_stay = partial_rows(jobs, (listed, listed_other), ranks, sides)

    early_stay, early_turn, vector = turn_near(early_stay, vector, early_code)
    early_code = send(early_turn, EARLY_FAR)
    late, late_turn = turn_y(late_stay, late_code, 16, LATE_FAR)
    near_code = send(late_turn, NEAR)
    later, later_turn = turn_y(later_stay, later_code, 0, LATER_FAR)
    late, late_turn = turn_z(late, near_code, 0)
    late_code = send(late_turn, LATE_FAR)
    later, later_turn = turn_z(later, send(later_turn, NEAR), 0)
    later_code = send(later_turn, LATER_FAR)

    early_own, early_turn, vector, extra = turn_far(early_stay, vector, early_code)
    early, *early_back, extra, vector = finish_early(early_own, vector, extra, send(early_turn, Y))
    came = return_all(early_back, Z_FIRST)
    extra_core = send(extra, CORE)
    fitted, coulomb = coulomb_tile(vector, metric_inv, three_index)

    late, coulomb = lax.optimization_barrier((late, coulomb))
    late, *back = finish_late(late, late_code, SOONER)
    came += return_all(back, SOONER)
    later, *back = finish_late(later, later_code, LATER)
    came += return_all(back, LATER)
    exchange = assemble(row_block, early, late, later, extra, extra_core, *came)
    return (exchange, coulomb, fitted[0])


def solution(mesh):
    placed = (
        P(("groups", "row"), None, None, None),
        P(("groups", "row"), None),
        P("groups"),
        P(("groups", "row"), None, None),
        P("groups", None),
        P(("groups", "row"), None, None, None),
    )
    return jax.shard_map(
        summed_rows if mesh.shape["row"] == ROWS else sent_panels,
        mesh=mesh,
        in_specs=placed,
        out_specs=(P(("groups", "row"), None, None), P(("groups", "row"), None, None), P("groups")),
        check_vma=False,
    )
```

```python
import functools
import jax
import jax.numpy as jnp
from jax import lax
from jax.experimental import pallas as pl
from jax.experimental.pallas import tpu as pltpu
from jax.sharding import PartitionSpec as P


def row_terms(rows_in, row_ids, owned, count):
    total_rows = rows_in.shape[0]
    group = 32
    slots = rows_in.shape[1]
    width = rows_in.shape[3]
    grouped = rows_in.reshape((total_rows // group, group) + rows_in.shape[1:])
    grouped_ids = row_ids.reshape(total_rows // group, group, slots)

    def step(total, item):
        block_rows, block_ids = item
        chosen = (block_ids == owned).astype(jnp.bfloat16)
        picked = jnp.einsum(
            "gs,gspk->gpk", chosen, block_rows, preferred_element_type=jnp.float32
        ).astype(jnp.bfloat16)
        prods = jnp.einsum("gpk,gspn->gskn", picked, block_rows, preferred_element_type=jnp.float32)
        target = jnp.maximum(block_ids, 0).reshape(-1)
        added = jax.ops.segment_sum(prods.reshape(-1, width, width), target, num_segments=count)
        return (total + added, None)

    start = jnp.zeros((count, width, width), jnp.float32)
    total, _ = lax.scan(step, start, (grouped, grouped_ids))
    return total


def sent_panels(panels, blocks, row_block, coeffs, metric_inv, three_index):
    count = row_block.shape[0]
    orbits, slots, aux, width = panels.shape
    capacity = max(2, (orbits * slots + count - 1) // count)
    here = lax.axis_index("row")
    owned = row_block[here]
    ranks = jnp.arange(count, dtype=jnp.int32)
    flat_ids = blocks.reshape(-1)
    matches = (row_block[None, :] == flat_ids[:, None]).astype(jnp.int32)
    target = jnp.sum(matches * ranks[None, :], axis=1)
    hits = (ranks[None, :] == target[:, None]).astype(jnp.int32)
    before = jnp.cumsum(hits, axis=0) - hits
    place = jnp.sum(before * hits, axis=1)
    source = jnp.repeat(panels, slots, axis=0)
    source_ids = jnp.repeat(blocks, slots, axis=0).astype(jnp.bfloat16)
    outgoing = (
        jnp.zeros((count, capacity, slots, aux, width), jnp.bfloat16).at[target, place].set(source)
    )
    outgoing_ids = (
        jnp.full((count, capacity, slots), -1.0, jnp.bfloat16).at[target, place].set(source_ids)
    )
    partial_terms = jnp.einsum(
        "ispm,ism->p", panels.astype(jnp.float32), coeffs, precision=lax.Precision.HIGHEST
    )
    gamma = lax.psum(partial_terms, "row")
    fitted = jnp.dot(metric_inv, gamma, precision=lax.Precision.HIGHEST)
    coulomb = jnp.einsum(
        "p,rpmn->rmn", fitted, three_index.astype(jnp.float32), precision=lax.Precision.HIGHEST
    )
    arrived, arrived_ids = (
        lax.all_to_all(outgoing, "row", split_axis=0, concat_axis=0, tiled=True),
        lax.all_to_all(outgoing_ids, "row", split_axis=0, concat_axis=0, tiled=True),
    )
    accum = row_terms(
        arrived.reshape(-1, slots, aux, width),
        arrived_ids.reshape(-1, slots).astype(jnp.int32),
        owned,
        count,
    )
    exchange = accum.transpose(1, 0, 2).reshape(width, count * width)[None].astype(jnp.bfloat16)
    return (exchange, coulomb.astype(jnp.bfloat16), fitted)


ROWS = 16
CORE, Y, Z = 1, 2, (4, 8, 12)
NEAR = 4
EARLY_FAR, LATE_FAR, LATER_FAR = 8, 12, 12
PLACES = 16
Z_FIRST, SOONER, LATER = (3, "extra"), (1, "diagonal"), (2, "mate")
TAIL = 16
TOP = 14.99
SPARE = 0
VECTOR = 4
AHEAD = 8
SHORT = pl.CostEstimate(flops=1024, bytes_accessed=1024, transcendentals=0)
LONG = pl.CostEstimate(flops=1 << 32, bytes_accessed=1024, transcendentals=0)


def send(x, flip):
    return lax.ppermute(x, "row", [(i, i ^ flip) for i in range(ROWS)])


def side_of(z, apart):
    return (z >> 1) & 1 if apart == 2 else z & 1


def first_place(row, region):
    if region in ("diagonal", "mate"):
        return int(region == "mate")
    if region == "extra":
        return 2 + ((row >> 1) & 1)
    return region * 4 + side_of(row >> 2, region) * 2


def returned(group):
    return [region for region in group if region in (1, 2, 3)]


EXTRA_SPARE = 48


def spare_of(region):
    return {Z_FIRST[0]: 32, SOONER[0]: 16, LATER[0]: 0}[region]


def width_of(region):
    return 2 if region in (1, 2, 3) else 1


def encode_row(out, j, x, tail):
    height, columns = x.shape
    if tail is None:
        tail = jnp.zeros((out.shape[0] % height, columns), jnp.float32)
    peak = jnp.maximum(jnp.max(jnp.abs(x), axis=0, keepdims=True), 2.0**-100)
    exponent = jnp.ceil(jnp.log2(peak) * 8)
    scaled = jnp.round(x * jnp.exp2(TOP - exponent * 0.125))
    out[j * height : (j + 1) * height, :] = scaled.astype(jnp.int32).astype(jnp.int16)
    return jnp.where(lax.broadcasted_iota(jnp.int32, tail.shape, 0) == j, exponent, tail)


def encode_tail(out, tail, vector=()):
    rest, columns = tail.shape
    line = lax.broadcasted_iota(jnp.int32, tail.shape, 0)
    for j, x in enumerate(vector):
        beside = jnp.zeros((1, columns - x.shape[1]), jnp.float32)
        tail = jnp.where(line == VECTOR + j, jnp.concatenate([x, beside], axis=1), tail)
    out[out.shape[0] - rest :, :] = tail.astype(jnp.int32).astype(jnp.int16)


def encode(out, sums, vector=()):
    tail = None
    for j, x in enumerate(sums):
        tail = encode_row(out, j, x, tail)
    encode_tail(out, tail, vector)


def encode_vector(x):
    exponent = jnp.ceil(jnp.log2(jnp.maximum(jnp.abs(x), 2.0**-100)))
    scaled = x * jnp.exp2(14 - exponent)
    high = jnp.round(scaled)
    low = jnp.round((scaled - high) * 2.0**15)
    return (exponent, high, low), combine(exponent, high, low)


def combine(exponent, high, low):
    return (high + low * 2.0**-15) * jnp.exp2(exponent - 14)


def decode_vector(codes, width):
    tail = codes[codes.shape[0] - TAIL :, :width].astype(jnp.int32).astype(jnp.float32)
    return combine(*(tail[VECTOR + j : VECTOR + j + 1, :] for j in range(3)))


def decode(codes, j, height):
    count = (codes.shape[0] - TAIL) // height
    exponents = codes[count * height :, :].astype(jnp.int32).astype(jnp.float32)
    scale = jnp.exp2(exponents[j : j + 1, :] * 0.125 - TOP)
    return codes[j * height : (j + 1) * height, :].astype(jnp.int32).astype(jnp.float32) * scale


def bring_kernel(far, near, arrived):
    copy = pltpu.make_async_copy(far, near, arrived)
    copy.start()
    copy.wait()


def bring(panels):
    return pl.pallas_call(
        bring_kernel,
        in_specs=[pl.BlockSpec(memory_space=pltpu.HBM)],
        out_specs=pl.BlockSpec(memory_space=pltpu.VMEM),
        out_shape=jax.ShapeDtypeStruct(panels.shape, panels.dtype),
        scratch_shapes=[pltpu.SemaphoreType.DMA],
        compiler_params=pltpu.CompilerParams(vmem_limit_bytes=16 << 20),
        cost_estimate=SHORT,
    )(panels)


def density_of(panels, coeffs):
    orbits, slots, aux, width = panels.shape
    total = jnp.zeros((aux, width), jnp.float32)
    for i in range(orbits):
        for t in range(slots):
            total = total + panels[i, t].astype(jnp.float32) * coeffs[t, i : i + 1, :]
    return total


def rows_kernel(jobs, project, listed, ranks, listed_other, ranks_other, mine, other_far, *refs):
    if project:
        coeffs, coeffs_other, refs = refs[0], refs[1], refs[2:]
    outs, (other, arrived), picks, spreads = refs[: -2 * AHEAD - 2], refs[-2:], refs[-2 * AHEAD - 2 : -AHEAD - 2], refs[-AHEAD - 2 : -2]
    orbits, slots, aux, width = mine.shape
    capacity = listed.shape[1]
    me = lax.axis_index("row")
    copy = pltpu.make_async_copy(other_far, other, arrived)
    copy.start()
    todo = [(job, j) for job in range(len(jobs)) for j in range(len(jobs[job][1]))]

    def spans_of(job, j):
        groups, flips, _ = jobs[job]
        return [
            [
                pl.ds(pl.multiple_of(first_place(me ^ flips[j], region) * width, width), width_of(region) * width)
                for region in group
            ]
            for group in groups
        ]

    def gather(step, side):
        job, j = todo[step]
        row = me ^ jobs[job][1][j]
        picked, spread = picks[step % AHEAD], spreads[step % AHEAD]
        names, places_of, panels = ((listed, ranks, mine), (listed_other, ranks_other, other))[side]
        half = capacity * aux
        for span in sum(spans_of(job, j), []):
            spread[side * half : (side + 1) * half, span] = jnp.zeros((half, span.size), jnp.bfloat16)
        for n in range(capacity):
            code = names[row, n]
            orbit, slot = jnp.maximum(code, 0) >> 3, jnp.maximum(code, 0) & 7
            at = pl.ds((side * capacity + n) * aux, aux)
            chosen = panels[orbit, slot]
            tiles = [panels[orbit, t] for t in range(slots)]
            places = [places_of[t, orbit] ^ row for t in range(slots)]
            picked[at, :] = jnp.where(code >= 0, chosen, jnp.zeros_like(chosen))
            for tile, place in zip(tiles, places):
                spread[at, pl.ds(pl.multiple_of(place * width, width), width)] = tile

    for step in range(min(AHEAD, len(todo))):
        gather(step, 0)
    if project:
        total = density_of(mine, coeffs)
    copy.wait()
    vector = ()
    if project:
        total = jnp.sum((total + density_of(other, coeffs_other)).T, axis=0, keepdims=True)
        total = jnp.concatenate([total, jnp.zeros((1, width - aux), jnp.float32)], axis=1)
        vector, outs[-1][...] = encode_vector(total)
    first, tails = 0, {}
    for step, (job, j) in enumerate(todo):
        gather(step, 1)
        picked, spread = picks[step % AHEAD], spreads[step % AHEAD]
        sums = [
            [
                lax.dot_general(
                    picked[...],
                    spread[:, span],
                    (((0,), (0,)), ((), ())),
                    preferred_element_type=jnp.float32,
                )
                for span in spans
            ]
            for spans in spans_of(job, j)
        ]
        if step + AHEAD < len(todo):
            gather(step + AHEAD, 0)
        groups, flips, coded = jobs[job]
        for k, parts in enumerate(sums):
            out = outs[first + k]
            row = jnp.concatenate(parts, axis=1) if len(parts) > 1 else parts[0]
            if not coded:
                out[j] = row
                continue
            tails[job, k] = encode_row(out, j, row, tails.get((job, k)))
            if j + 1 == len(flips):
                encode_tail(out, tails[job, k], vector if job + 1 == len(jobs) else ())
        if j + 1 == len(flips):
            first += len(groups)


def partial_rows(jobs, lists, ranks, panels, *coeffs):
    orbits, slots, aux, width = panels[0].shape
    depth = 2 * lists[0].shape[1] * aux
    shapes = []
    for groups, flips, coded in jobs:
        for group in groups:
            columns = sum(width_of(region) for region in group) * width
            if coded:
                spare = SPARE if group == LATER else 0
                shapes.append(message_of(len(flips) * width, columns, spare))
            else:
                shapes.append(sums_of(len(flips), width, columns))
    if coeffs:
        shapes.append(jax.ShapeDtypeStruct((1, width), jnp.float32))
    scalars = pl.BlockSpec(memory_space=pltpu.SMEM)
    whole = pl.BlockSpec(memory_space=pltpu.VMEM)
    return pl.pallas_call(
        functools.partial(rows_kernel, jobs, len(coeffs)),
        in_specs=[scalars] * 4 + [whole, pl.BlockSpec(memory_space=pltpu.HBM)] + [whole] * len(coeffs),
        out_specs=[whole] * len(shapes),
        out_shape=shapes,
        scratch_shapes=[pltpu.VMEM((depth, width), jnp.bfloat16)] * AHEAD
        + [pltpu.VMEM((depth, PLACES * width), jnp.bfloat16)] * AHEAD
        + [pltpu.VMEM(panels[1].shape, jnp.bfloat16), pltpu.SemaphoreType.DMA],
        compiler_params=pltpu.CompilerParams(vmem_limit_bytes=40 << 20),
        cost_estimate=SHORT,
    )(lists[0], ranks[0], lists[1], ranks[1], *panels, *coeffs)


def turn_y_kernel(last, stay, code, kept, message):
    height = stay.shape[1]
    encode(message, [stay[j] + decode(code, j, height) for j in (1, 1 ^ last // 4)])
    for k, j in enumerate((0, last // 4)):
        kept[k] = stay[j] + decode(code, j, height)


def turn_z_kernel(kept, code, own, message):
    height = own.shape[0]
    encode(message, [kept[1] + decode(code, 1, height)])
    own[...] = kept[0] + decode(code, 0, height)


def turn_near_kernel(stay, projected, code, kept, message, vector):
    height = kept.shape[1]
    rows, vector[...] = encode_vector(projected[...] + decode_vector(code, projected.shape[1]))
    encode(message, [stay[j] + decode(code, j, height) for j in (2, 3)], rows)
    for j in range(2):
        kept[j] = stay[j] + decode(code, j, height)


def turn_far_kernel(stay, projected, code, own, message, vector, extra):
    height, width = own.shape[0], extra.shape[1]
    rows, vector[...] = encode_vector(projected[...] + decode_vector(code, projected.shape[1]))
    theirs, mine = [stay[j] + decode(code, j, height) for j in range(2)]
    encode(message, [jnp.concatenate([theirs, mine[:, -width:]], axis=1)], rows)
    own[...] = mine
    extra[...] = theirs[:, -width:]


def message_of(rows, columns, spare=0):
    return jax.ShapeDtypeStruct((rows + TAIL + spare, columns), jnp.int16)


def small_call(kernel, shapes, *args, cost=SHORT):
    return pl.pallas_call(
        kernel,
        out_shape=shapes,
        compiler_params=pltpu.CompilerParams(vmem_limit_bytes=16 << 20),
        cost_estimate=cost,
    )(*args)


def sums_of(*shape):
    return jax.ShapeDtypeStruct(shape, jnp.float32)


def turn_y(stay, code, spare, last):
    height, columns = stay.shape[1:]
    shapes = [sums_of(2, height, columns), message_of(2 * height, columns, spare)]
    return small_call(functools.partial(turn_y_kernel, last), shapes, stay, code)


def turn_z(kept, code, spare):
    height, columns = kept.shape[1:]
    shapes = [sums_of(height, columns), message_of(height, columns, spare)]
    return small_call(turn_z_kernel, shapes, kept, code)


def turn_near(stay, projected, code):
    height, columns = stay.shape[1:]
    shapes = [sums_of(2, height, columns), message_of(2 * height, columns), sums_of(1, projected.shape[1])]
    return small_call(turn_near_kernel, shapes, stay, projected, code)


def turn_far(stay, projected, code):
    height, columns = stay.shape[1:]
    shapes = [sums_of(height, columns), message_of(height, columns + height), sums_of(*projected.shape)]
    shapes.append(sums_of(height, height))
    return small_call(turn_far_kernel, shapes, stay, projected, code)


def coulomb_kernel(vector, metric, tiles, fitted, out):
    aux, height, width = tiles.shape[1:]
    column = jnp.sum(metric[...] * vector[0:1, :aux], axis=1, keepdims=True)
    fitted[...] = jnp.broadcast_to(column, (aux, width)).T[0:1, :]
    total = jnp.zeros((height, width), jnp.float32)
    for p in range(aux):
        total = total + column[p : p + 1, 0:1] * tiles[0, p].astype(jnp.float32)
    out[0] = total.astype(jnp.bfloat16)


def coulomb_tile(vector, metric_inv, three_index):
    aux, height, width = three_index.shape[1:]
    return pl.pallas_call(
        coulomb_kernel,
        out_shape=[
            jax.ShapeDtypeStruct((1, aux), jnp.float32),
            jax.ShapeDtypeStruct((1, height, width), jnp.bfloat16),
        ],
        compiler_params=pltpu.CompilerParams(vmem_limit_bytes=16 << 20),
        cost_estimate=SHORT,
    )(vector, metric_inv, three_index)


def finish_row(total, done, *backs):
    height = total.shape[0]
    done[...] = total.astype(jnp.bfloat16)
    for k, out in enumerate(backs):
        for b in range(2):
            at = (2 * k + b) * height
            out[b * height : (b + 1) * height, :] = total[:, at : at + height].T.astype(jnp.bfloat16)
        if out.shape[0] > 2 * height:
            out[2 * height :, :] = jnp.zeros((out.shape[0] - 2 * height, height), jnp.bfloat16)


def backs_of(group, height):
    return [
        jax.ShapeDtypeStruct((2 * height + spare_of(region), height), jnp.bfloat16)
        for region in returned(group)
    ]


def finish_early_kernel(own, vector, extra, code, done, *refs):
    height, columns = own.shape
    *backs, other_extra, vector_out = refs
    came = decode(code, 0, height)
    finish_row(own[...] + came[:, :columns], done, *backs)
    other_extra[:height, :] = (extra[...] + came[:, columns:]).T.astype(jnp.bfloat16)
    other_extra[height:, :] = jnp.zeros((other_extra.shape[0] - height, height), jnp.bfloat16)
    vector_out[...] = vector[...] + decode_vector(code, vector.shape[1])


def finish_early(own, vector, extra, code):
    height = own.shape[0]
    shapes = [jax.ShapeDtypeStruct(own.shape, jnp.bfloat16)] + backs_of(Z_FIRST, height)
    shapes += [jax.ShapeDtypeStruct((2 * height + EXTRA_SPARE, height), jnp.bfloat16), sums_of(*vector.shape)]
    return small_call(finish_early_kernel, shapes, own, vector, extra, code)


def finish_late_kernel(own, code, done, *backs):
    finish_row(own[...] + decode(code, 0, own.shape[0]), done, *backs)


def finish_late(own, code, group, cost=SHORT):
    backs = backs_of(group, own.shape[0])
    return small_call(finish_late_kernel, [jax.ShapeDtypeStruct(own.shape, jnp.bfloat16)] + backs, own, code, cost=cost)


def give_back(blocks, region):
    came = lax.ppermute(blocks, "row", [(i, i ^ first_place(i, region)) for i in range(ROWS)])
    return came, send(came, CORE)


def return_all(backs, group):
    return sum((give_back(blocks, region) for blocks, region in zip(backs, returned(group))), ())


def assemble_kernel(holders, early, late, later, extra, extra_core, *refs):
    came, out = refs[:-1], refs[-1]
    width = early.shape[0]
    me = lax.axis_index("row")

    def put(place, block):
        where = pl.ds(pl.multiple_of(holders[place ^ me] * width, width), width)
        out[0, :, where] = block

    k = 0
    for group, rows in ((Z_FIRST, early), (SOONER, late), (LATER, later)):
        at = 0
        for region in group:
            start = first_place(me, region)
            for b in range(width_of(region)):
                put(start + b, rows[:, at * width : (at + 1) * width])
                at += 1
            if region in returned(group):
                start = region * 8 + 2 - start
                put(start, came[k][:width, :])
                put(start + 1, came[k + 1][width : 2 * width, :])
                k += 2
    put(5 - first_place(me, "extra"), jnp.where((me >> 1) & 1 == 0, extra_core[:width, :], extra[:width, :]))


def assemble(row_block, early, *rest):
    width = early.shape[0]
    vmem = pl.BlockSpec(memory_space=pltpu.VMEM)
    return pl.pallas_call(
        assemble_kernel,
        in_specs=[pl.BlockSpec(memory_space=pltpu.SMEM)] + [vmem] * (1 + len(rest)),
        out_shape=jax.ShapeDtypeStruct((1, width, ROWS * width), jnp.bfloat16),
        compiler_params=pltpu.CompilerParams(vmem_limit_bytes=16 << 20),
        cost_estimate=SHORT,
    )(row_block, early, *rest)


def naming(blocks, row_block, capacity):
    slots, orbits = blocks.shape
    holders = jnp.arange(ROWS, dtype=jnp.int32)
    hits = (blocks[:, :, None] == row_block[None, None, :]).astype(jnp.int32)
    rank = jnp.sum(hits * holders, axis=2)
    named = jnp.sum(hits, axis=0)
    code = jnp.arange(orbits, dtype=jnp.int32)[:, None] * 8 + jnp.sum(
        hits * jnp.arange(slots, dtype=jnp.int32)[:, None, None], axis=0
    )
    earlier = (jnp.arange(orbits)[None, :] < jnp.arange(orbits)[:, None]).astype(jnp.int32)
    before = jnp.sum(earlier[:, :, None] * named[None, :, :], axis=1)
    here = (before[:, :, None] == jnp.arange(capacity)) & (named[:, :, None] > 0)
    listed = jnp.sum(jnp.where(here, code[:, :, None] + 1, 0), axis=0) - 1
    return listed, rank


def summed_rows(panels, blocks, row_block, coeffs, metric_inv, three_index):
    orbits, slots, aux, width = panels.shape
    capacity = orbits * slots // ROWS

    other = send(panels, CORE)
    coeffs = coeffs.transpose(1, 0, 2)
    coeffs_other = send(coeffs, CORE)
    listed, rank = naming(blocks.T, row_block, capacity)
    listed_other, rank_other = send(listed, CORE), send(rank, CORE)
    listed, rank, panels = lax.optimization_barrier((listed, rank, panels))
    mine = bring(panels)
    ranks, sides = (rank, rank_other), (mine, other)

    jobs = ((SOONER, LATER), [Y] + [z | Y for z in Z], True), ((Z_FIRST,), [4 | Y, 4, (4 ^ EARLY_FAR) | Y, 4 ^ EARLY_FAR], True)
    late_go, later_go, early_go, vector = partial_rows(
        jobs, (listed, listed_other), ranks, sides, coeffs, coeffs_other
    )
    late_code = send(late_go, Y)
    early_code = send(early_go, NEAR)
    later_code = send(later_go, Y)

    listed, *_ = lax.optimization_barrier((listed, late_go, early_go, later_go))
    jobs = ((Z_FIRST,), [Y, 0, EARLY_FAR | Y, EARLY_FAR], False), ((SOONER, LATER), [0, *Z], False)
    early_stay, late_stay, later_stay = partial_rows(jobs, (listed, listed_other), ranks, sides)

    early_stay, early_turn, vector = turn_near(early_stay, vector, early_code)
    early_code = send(early_turn, EARLY_FAR)
    late, late_turn = turn_y(late_stay, late_code, 16, LATE_FAR)
    near_code = send(late_turn, NEAR)
    later, later_turn = turn_y(later_stay, later_code, 0, LATER_FAR)
    late, late_turn = turn_z(late, near_code, 0)
    late_code = send(late_turn, LATE_FAR)
    later, later_turn = turn_z(later, send(later_turn, NEAR), 0)
    later_code = send(later_turn, LATER_FAR)

    early_own, early_turn, vector, extra = turn_far(early_stay, vector, early_code)
    early, *early_back, extra, vector = finish_early(early_own, vector, extra, send(early_turn, Y))
    came = return_all(early_back, Z_FIRST)
    extra_core = send(extra, CORE)
    fitted, coulomb = coulomb_tile(vector, metric_inv, three_index)

    late, coulomb = lax.optimization_barrier((late, coulomb))
    late, *back = finish_late(late, late_code, SOONER)
    came += return_all(back, SOONER)
    later, *back = finish_late(later, later_code, LATER)
    came += return_all(back, LATER)
    exchange = assemble(row_block, early, late, later, extra, extra_core, *came)
    return (exchange, coulomb, fitted[0])


def solution(mesh):
    placed = (
        P(("groups", "row"), None, None, None),
        P(("groups", "row"), None),
        P("groups"),
        P(("groups", "row"), None, None),
        P("groups", None),
        P(("groups", "row"), None, None, None),
    )
    return jax.shard_map(
        summed_rows if mesh.shape["row"] == ROWS else sent_panels,
        mesh=mesh,
        in_specs=placed,
        out_specs=(P(("groups", "row"), None, None), P(("groups", "row"), None, None), P("groups")),
        check_vma=False,
    )
```
